32 devices in a mesh: pole: 2 (over x), row: 4 (over y, core), col: 4 (over z).
Axes of the slice: x: 2, y: 2, z: 4, core: 2. Of those that a mesh axis runs over, the one named last changes fastest.
Arguments:
- known_inverse: float32 [4096, 2048], P(('pole', 'row'), 'col'), parts along dimension 0, may hold values from -1 to 2.5, as said below
- lower_first: float32 [4096, 512], P(('pole', 'row'), 'col'), parts along dimension 0, may hold values from -0.12 to 0.12
- lower_second: float32 [4096, 512], P(('pole', 'row'), 'col'), parts along dimension 0, may hold values from -0.12 to 0.12
- lower_third: float32 [4096, 512], P(('pole', 'row'), 'col'), parts along dimension 0, may hold values from -0.12 to 0.12
- ancestor: float32 [8, 3, 128, 128], P(('pole', 'col')), parts along dimension 0, may hold values from -0.6 to 0.6
- diag_inverse: float32 [6, 4, 128, 128], P('pole', 'col'), parts along dimension 0, may hold values from -1 to 2.5, as said below
- structure: int32 [4, 8], replicated, may hold values from 0 to 15, as said below
- pick_second: int32 [4, 7], replicated, may hold values from 0 to 7, as said below
- pick_third: int32 [4, 6], replicated, may hold values from 0 to 6, as said below
Outputs:
- first_cols: float32 [4096, 512], P(('pole', 'row'), 'col'), parts along dimension 0
- second_cols: float32 [4096, 512], P(('pole', 'row'), 'col'), parts along dimension 0
- third_cols: float32 [4096, 512], P(('pole', 'row'), 'col'), parts along dimension 0
- ancestral: float32 [8, 3, 128, 128], P(('pole', 'col')), parts along dimension 0
- diagonal: float32 [6, 4, 128, 128], P('pole', 'col'), parts along dimension 0
The draws below stay inside these ranges and needn't reach their ends.
There are 2 independent parts, one for each index of `pole`. The reference program is written for one: setup_inputs(seed, part) draws one part's arguments, and reference() takes and returns one part's arrays. A program takes and returns all parts, laid end to end along the dimension named above; an argument that names none is the same for every part. Nothing has to cross between parts.
Inputs may be any that keep to these rules, and one draw needn't show every extreme that they name: `structure`: each row names 8 different separator blocks. `pick_second`: each row names 7 different positions. `pick_third`: each row names 6 different positions. `known_inverse`: exactly symmetric. Every block diag_inverse[l, k] is exactly symmetric.
All inputs are finite; a program needn't handle non-finite values.
Results may differ from the reference program's by a relative error of at most 0.000071.
Values sent between devices are 32-bit elements; how exact they have to be, the bound alone decides.
A program may use at most 128 MiB of HBM per device.

```python
import jax
import jax.numpy as jnp
from jax import lax

B = 128
LEVELS = 3
NS = 16
N = 2048
M = 4
R1 = 8
R2 = 7
R3 = 6


def draw_known_inverse(key, part):
    key = jax.random.fold_in(key, 11)
    order = NS * B
    noise = jax.random.normal(key, (order, order), jnp.float32)
    return (noise + noise.T) * 0.035355339 + 1.5 * jnp.eye(order, dtype=jnp.float32)


def draw_diag_inverse(key, part):
    key = jax.random.fold_in(key, 12)
    noise = jax.random.normal(key, (LEVELS, M, B, B), jnp.float32)
    return (noise + jnp.swapaxes(noise, 2, 3)) * 0.070710678 + jnp.eye(B, dtype=jnp.float32)


def distinct_positions(key, row_total, count, chosen):
    noise = jax.random.randint(key, (row_total, count), 0, 1048576)
    scores = noise * count + jnp.arange(count, dtype=jnp.int32)[None, :]
    return lax.top_k(scores, chosen)[1].astype(jnp.int32)


def draw_structure(key, part):
    key = jax.random.fold_in(key, 13)
    favour_key, noise_key = jax.random.split(key)
    favour = jax.random.randint(favour_key, (NS,), 0, 2) * 16384
    noise = jax.random.randint(noise_key, (M, NS), 0, 65536)
    scores = (noise + favour[None, :]) * NS + jnp.arange(NS, dtype=jnp.int32)[None, :]
    return lax.top_k(scores, R1)[1].astype(jnp.int32)


def draw_pick_second(key, part):
    key = jax.random.fold_in(key, 14)
    return distinct_positions(key, M, R1, R2)


def draw_pick_third(key, part):
    key = jax.random.fold_in(key, 15)
    return distinct_positions(key, M, R2, R3)


def shard_levels(own_key, extent, cuts, least, largest):
    def one(axis_at, blocks):
        heights = jax.random.uniform(jax.random.fold_in(jax.random.fold_in(own_key, 6), axis_at), (blocks,), jnp.float32, least / len(cuts), largest / len(cuts))
        return jnp.repeat(jnp.exp(heights), extent[axis_at] // blocks).reshape((-1,) + (1,) * (len(extent) - axis_at - 1))

    gain = one(*cuts[0])
    for cut in cuts[1:]:
        gain = gain * one(*cut)
    return gain


def normal_values(own_key, extent, width, bound, cuts=(), held_as=jnp.bfloat16):
    drawn = jax.random.normal(own_key, extent, jnp.float32) * width
    if len(cuts) > 0:
        drawn = shard_levels(own_key, extent, cuts, -0.22, 0.18) * drawn
    return jnp.clip(drawn, min=-bound, max=bound).astype(held_as)


def setup_inputs(seed: int = 0, part: int = 0) -> dict:
    streams_of = jax.random.split(jax.random.key(seed), 10)
    part_keys = jax.random.split(jax.random.fold_in(streams_of[9], part), 10)
    known_inverse = draw_known_inverse(jax.random.fold_in(jax.random.fold_in(streams_of[9], part), 71), part)
    lower_first = normal_values(part_keys[1], (N, M * B), 0.02, 0.12, ((0, 4), (1, 4)), jnp.float32)
    lower_second = normal_values(part_keys[2], (N, M * B), 0.02, 0.12, ((0, 4), (1, 4)), jnp.float32)
    lower_third = normal_values(part_keys[3], (N, M * B), 0.02, 0.12, ((0, 4), (1, 4)), jnp.float32)
    ancestor = normal_values(part_keys[4], (M, LEVELS, B, B), 0.1, 0.6, ((0, 4),), jnp.float32)
    diag_inverse = draw_diag_inverse(jax.random.fold_in(jax.random.fold_in(streams_of[9], part), 71), part)
    structure = draw_structure(jax.random.fold_in(streams_of[9], 71), part)
    pick_second = draw_pick_second(jax.random.fold_in(streams_of[9], 71), part)
    pick_third = draw_pick_third(jax.random.fold_in(streams_of[9], 71), part)
    return {"known_inverse": known_inverse, "lower_first": lower_first, "lower_second": lower_second, "lower_third": lower_third, "ancestor": ancestor, "diag_inverse": diag_inverse, "structure": structure, "pick_second": pick_second, "pick_third": pick_third}


HIGHEST = lax.Precision.HIGHEST


def block_mask(members, block_count):
    block_ids = jnp.arange(block_count, dtype=jnp.int32)
    return jnp.sum((members[:, :, None] == block_ids[None, None, :]).astype(jnp.float32), axis=1)


def structure_masks(structure, pick_second, pick_third, block_count):
    second_ids = jnp.take_along_axis(structure, pick_second, axis=1)
    third_ids = jnp.take_along_axis(second_ids, pick_third, axis=1)
    return (block_mask(structure, block_count), block_mask(second_ids, block_count), block_mask(third_ids, block_count))


def expand_mask(mask_table, block_size):
    return jnp.repeat(jnp.repeat(mask_table.T, block_size, axis=0), block_size, axis=1)


def node_times(columns, blocks):
    height = columns.shape[0]
    node_count = blocks.shape[0]
    block_size = blocks.shape[1]
    reshaped = columns.reshape(height, node_count, block_size)
    return jnp.einsum("rkb,kbc->rkc", reshaped, blocks, precision=HIGHEST).reshape(height, node_count * block_size)


def node_inner(former, latter, block_size):
    height = former.shape[0]
    node_count = former.shape[1] // block_size
    return jnp.einsum("rkb,rkc->kbc", former.reshape(height, node_count, block_size), latter.reshape(height, node_count, block_size), precision=HIGHEST)


def block_product(former, latter):
    return jnp.einsum("kbc,kcd->kbd", former, latter, precision=HIGHEST)


def block_tproduct(former, latter):
    return jnp.einsum("kcb,kcd->kbd", former, latter, precision=HIGHEST)


def reference(known_inverse, lower_first, lower_second, lower_third, ancestor, diag_inverse, structure, pick_second, pick_third):
    block_count = known_inverse.shape[0] // B
    masks = structure_masks(structure, pick_second, pick_third, block_count)
    expanded = [expand_mask(mask_table, B) for mask_table in masks]
    lowers = [factor * kept_rows for factor, kept_rows in zip((lower_first, lower_second, lower_third), expanded)]
    products = [jnp.dot(known_inverse, masked, precision=HIGHEST) for masked in lowers]
    link_two = ancestor[:, 0]
    link_near = ancestor[:, 1]
    link_far = ancestor[:, 2]
    first_cols = -expanded[0] * products[0]
    diag_first = diag_inverse[0] - node_inner(lowers[0], first_cols, B)
    second_cols = -expanded[1] * (products[1] + node_times(first_cols, link_two))
    cross_two = -(node_inner(first_cols, lowers[1], B) + block_product(diag_first, link_two))
    diag_second = diag_inverse[1] - node_inner(lowers[1], second_cols, B) - block_tproduct(link_two, cross_two)
    third_cols = -expanded[2] * (products[2] + node_times(second_cols, link_near) + node_times(first_cols, link_far))
    cross_near = -(node_inner(second_cols, lowers[2], B) + block_product(diag_second, link_near) + block_tproduct(cross_two, link_far))
    cross_far = -(node_inner(first_cols, lowers[2], B) + block_product(cross_two, link_near) + block_product(diag_first, link_far))
    diag_third = diag_inverse[2] - node_inner(lowers[2], third_cols, B) - block_tproduct(link_near, cross_near) - block_tproduct(link_far, cross_far)
    ancestral = jnp.stack([cross_two, cross_near, cross_far], axis=1)
    diagonal = jnp.stack([diag_first, diag_second, diag_third], axis=0)
    return first_cols, second_cols, third_cols, ancestral, diagonal
```

```python
import jax
import jax.numpy as jnp
from jax import lax
from jax.experimental import pallas as pl
from jax.experimental.pallas import tpu as pltpu
from jax.sharding import PartitionSpec as P

HIGHEST = lax.Precision.HIGHEST


def broadcast(array, axis, root):
    mine = lax.axis_index(axis) == root
    return lax.psum(jnp.where(mine, array, jnp.zeros_like(array)), axis)


def block_mask(members, block_count):
    block_ids = jnp.arange(block_count, dtype=jnp.int32)
    return jnp.sum((members[:, :, None] == block_ids[None, None, :]).astype(jnp.float32), axis=1)


def structure_masks(structure, pick_second, pick_third, block_count):
    second_ids = jnp.take_along_axis(structure, pick_second, axis=1)
    third_ids = jnp.take_along_axis(second_ids, pick_third, axis=1)
    return (
        block_mask(structure, block_count),
        block_mask(second_ids, block_count),
        block_mask(third_ids, block_count),
    )


def expand_mask(mask_table, block_size):
    return jnp.repeat(jnp.repeat(mask_table.T, block_size, axis=0), block_size, axis=1)


def node_times(columns, blocks):
    height = columns.shape[0]
    node_count = blocks.shape[0]
    block_size = blocks.shape[1]
    reshaped = columns.reshape(height, node_count, block_size)
    return jnp.einsum("rkb,kbc->rkc", reshaped, blocks, precision=HIGHEST).reshape(
        height, node_count * block_size
    )


def node_inner(former, latter, block_size):
    height = former.shape[0]
    node_count = former.shape[1] // block_size
    return jnp.einsum(
        "rkb,rkc->kbc",
        former.reshape(height, node_count, block_size),
        latter.reshape(height, node_count, block_size),
        precision=HIGHEST,
    )


def block_product(former, latter):
    return jnp.einsum("kbc,kcd->kbd", former, latter, precision=HIGHEST)


def block_tproduct(former, latter):
    return jnp.einsum("kcb,kcd->kbd", former, latter, precision=HIGHEST)


def row_total(partial_sum):
    return lax.psum(partial_sum, "row")


def on_device(
    known_inverse,
    lower_first,
    lower_second,
    lower_third,
    ancestor,
    diag_inverse,
    structure,
    pick_second,
    pick_third,
):
    block_size = ancestor.shape[2]
    row_group = lax.axis_size("row") // lax.axis_size("col")
    local_blocks = known_inverse.shape[0] // block_size
    block_count = local_blocks * lax.axis_size("row")
    local_nodes = ancestor.shape[0]
    masks = structure_masks(structure, pick_second, pick_third, block_count)
    block_start = lax.axis_index("row") * local_blocks
    node_start = lax.axis_index("col") * local_nodes
    expanded = [
        expand_mask(
            lax.dynamic_slice(mask_table, (node_start, block_start), (local_nodes, local_blocks)),
            block_size,
        )
        for mask_table in masks
    ]
    lowers = [
        factor * kept_rows
        for factor, kept_rows in zip((lower_first, lower_second, lower_third), expanded)
    ]
    products = []
    for masked in lowers:
        gathered = lax.all_gather(masked, "col", axis=1, tiled=True)
        pieces = [
            broadcast(gathered, "row", lax.axis_index("col") * row_group + offset)
            for offset in range(row_group)
        ]
        partial_value = jnp.dot(known_inverse, jnp.concatenate(pieces, axis=0), precision=HIGHEST)
        products.append(lax.psum_scatter(partial_value, "col", scatter_dimension=1, tiled=True))
    link_two = ancestor[:, 0]
    link_near = ancestor[:, 1]
    link_far = ancestor[:, 2]
    first_cols = -expanded[0] * products[0]
    diag_first = diag_inverse[0] - row_total(node_inner(lowers[0], first_cols, block_size))
    second_cols = -expanded[1] * (products[1] + node_times(first_cols, link_two))
    parent_part = lax.psum(node_inner(first_cols, lowers[1], block_size), "row")
    cross_two = -(parent_part + block_product(diag_first, link_two))
    diag_second = (
        diag_inverse[1]
        - row_total(node_inner(lowers[1], second_cols, block_size))
        - block_tproduct(link_two, cross_two)
    )
    third_cols = -expanded[2] * (
        products[2] + node_times(second_cols, link_near) + node_times(first_cols, link_far)
    )
    near_part, far_part = lax.psum(
        (
            node_inner(second_cols, lowers[2], block_size),
            node_inner(first_cols, lowers[2], block_size),
        ),
        "row",
    )
    cross_near = -(
        near_part + block_product(diag_second, link_near) + block_tproduct(cross_two, link_far)
    )
    cross_far = -(
        far_part + block_product(cross_two, link_near) + block_product(diag_first, link_far)
    )
    diag_third = (
        diag_inverse[2]
        - row_total(node_inner(lowers[2], third_cols, block_size))
        - block_tproduct(link_near, cross_near)
        - block_tproduct(link_far, cross_far)
    )
    ancestral = jnp.stack([cross_two, cross_near, cross_far], axis=1)
    diagonal = jnp.stack([diag_first, diag_second, diag_third], axis=0)
    return (first_cols, second_cols, third_cols, ancestral, diagonal)


SIDE = 4
BLOCK = 128
CHUNKS = 8
MESH = pl.DeviceIdType.MESH


def landing_plan():
    half = {
        (0, 0): [],
        (1, 0): [(2, 2, False), (3, 3, False), (1, 1, True)],
        (2, 0): [(2, 1, False)],
        (3, 0): [(2, 1, False), (3, 1, False)],
        (0, 1): [(0, 0, False)],
        (1, 1): [],
        (2, 1): [(0, 0, False), (2, 2, False)],
        (3, 1): [(0, 0, False), (2, 2, False), (3, 3, False)],
    }
    plan = {}
    for (row, col), slots in half.items():
        plan[row, col] = [(col, None, False)] + slots
        plan[3 - row, 3 - col] = [(3 - col, None, False)] + [
            (3 - other, 3 - source, late) for other, source, late in slots
        ]
    return plan


def transfers():
    plan = landing_plan()
    sends = {place: [] for place in plan}
    for (row, col), slots in plan.items():
        for slot, (other, source, late) in enumerate(slots):
            if slot == 0:
                continue
            held = [have[0] for have in plan[row, source]]
            assert other in held
            sends[row, source].append((held.index(other), (row, col), slot, late))
    return plan, sends


def lookup(me, values):
    total = jnp.int32(0)
    for place, value in values.items():
        if value:
            total = total + jnp.where(me == place[0] * SIDE + place[1], jnp.int32(value), jnp.int32(0))
    return total


def split(value):
    high = value.astype(jnp.bfloat16)
    low = (value - high.astype(jnp.float32)).astype(jnp.bfloat16)
    return high, low


def mul(a, b):
    return jnp.dot(a, b, preferred_element_type=jnp.float32)


def dot3(left, right):
    return mul(left[0], right[0]) + (mul(left[0], right[1]) + mul(left[1], right[0]))


def fused_kernel(
    structure_ref, second_ref, third_ref,
    k_ref, l1_ref, l2_ref, l3_ref, anc_ref, dinv_ref,
    first_ref, second_out, third_out, ancestral_ref, diagonal_ref,
    kbuf, mf, mhi, mlo, acc, outm, pin, part, got_core, half_sum, got_row, total,
    ksend, krecv, msend, mrecv, psend, precv, rsend, rrecv,
):
    row = lax.axis_index("row")
    col = lax.axis_index("col")
    me = row * SIDE + col
    plan, sends = transfers()
    levels = (l1_ref, l2_ref, l3_ref)
    rows_of = SIDE * BLOCK
    step_rows = rows_of // CHUNKS

    def at(place):
        return pl.when(me == place[0] * SIDE + place[1])

    def block_copy(index, source_slot, target, slot, chunk):
        rows = pl.ds(chunk * step_rows, step_rows)
        source = k_ref.at[rows] if source_slot == 0 else kbuf.at[source_slot - 1, rows]
        return pltpu.make_async_remote_copy(
            src_ref=source,
            dst_ref=kbuf.at[slot - 1, rows],
            send_sem=ksend.at[index, chunk],
            recv_sem=krecv.at[slot - 1, chunk],
            device_id={"col": target[1]},
            device_id_type=MESH,
        )

    def wait_block(slot, chunk):
        rows = pl.ds(chunk * step_rows, step_rows)
        pltpu.make_async_copy(k_ref.at[rows], kbuf.at[slot - 1, rows], krecv.at[slot - 1, chunk]).wait()

    def factor_copy(owner, taker):
        return pltpu.make_async_remote_copy(
            src_ref=mf.at[owner],
            dst_ref=mf.at[owner],
            send_sem=msend.at[taker],
            recv_sem=mrecv.at[owner],
            device_id={"row": taker},
            device_id_type=MESH,
        )

    def product_copy(sender, slot, taker):
        return pltpu.make_async_remote_copy(
            src_ref=outm.at[slot],
            dst_ref=pin.at[sender],
            send_sem=psend.at[slot],
            recv_sem=precv.at[sender],
            device_id={"row": taker},
            device_id_type=MESH,
        )

    barrier = pltpu.get_barrier_semaphore()
    for step in range(1, SIDE):
        pl.semaphore_signal(barrier, inc=1, device_id={"col": lax.rem(col + step, SIDE)}, device_id_type=MESH)
        pl.semaphore_signal(barrier, inc=1, device_id={"row": lax.rem(row + step, SIDE)}, device_id_type=MESH)
    pl.semaphore_wait(barrier, 2 * (SIDE - 1))

    for place, listed in sends.items():
        early = [(i, s) for i, s in enumerate(listed) if s[0] == 0 and not s[3]]
        if early:
            @at(place)
            def _(early=early):
                for chunk in range(CHUNKS):
                    for index, (source_slot, target, slot, _) in early:
                        block_copy(index, source_slot, target, slot, chunk).start()

    def marks(ids, block):
        total_mark = jnp.float32(0)
        for one in ids:
            total_mark = total_mark + jnp.where(one == block, jnp.float32(1), jnp.float32(0))
        return total_mark

    ids_1 = [structure_ref[col, i] for i in range(structure_ref.shape[1])]
    ids_2 = [structure_ref[col, second_ref[col, i]] for i in range(second_ref.shape[1])]
    ids_3 = [
        structure_ref[col, second_ref[col, third_ref[col, i]]] for i in range(third_ref.shape[1])
    ]
    keep = [[marks(ids, row * SIDE + i) for i in range(SIDE)] for ids in (ids_1, ids_2, ids_3)]
    for level in range(3):
        for i in range(SIDE):
            rows = slice(i * BLOCK, (i + 1) * BLOCK)
            columns = slice(level * BLOCK, (level + 1) * BLOCK)
            mf[row, rows, columns] = levels[level][rows, :] * keep[level][i]

    needs = {place: [] for place in plan}
    for (r, k), slots in plan.items():
        for slot, (other, _, _) in enumerate(slots):
            if other != r:
                needs[other, k].append((slot, r))
    for (b, k), takers in needs.items():
        if takers:
            @at((b, k))
            def _(b=b, takers=takers):
                for _, taker in sorted(takers):
                    factor_copy(b, taker).start()

    acc[...] = jnp.zeros_like(acc)

    def split_factor(index):
        def body(t, carry):
            rows = pl.ds(pl.multiple_of(t * BLOCK, BLOCK), BLOCK)
            high, low = split(mf[index, rows, :])
            mhi[index, rows, :] = high
            mlo[index, rows, :] = low
            return carry
        lax.fori_loop(0, SIDE, body, 0)

    split_factor(row)

    def relay(chunks):
        for place, listed in sends.items():
            passed = [(i, s) for i, s in enumerate(listed) if s[0] != 0]
            if passed:
                @at(place)
                def _(passed=passed):
                    for chunk in chunks:
                        for index, (source_slot, target, slot, _) in passed:
                            wait_block(source_slot, chunk)
                            block_copy(index, source_slot, target, slot, chunk).start()

    relay(range(0, CHUNKS // 2))

    def work(slot):
        has = lookup(me, {p: int(len(s) > slot) for p, s in plan.items()})
        other = lookup(me, {p: s[slot][0] for p, s in plan.items() if len(s) > slot})
        source = k_ref if slot == 0 else kbuf.at[slot - 1]
        if slot > 0:
            relayed = {
                p: int(any(s[0] == slot for s in listed)) for p, listed in sends.items()
            }
            fresh = has - lookup(me, relayed)

            @pl.when(fresh == 1)
            def _():
                for chunk in range(CHUNKS):
                    wait_block(slot, chunk)

        @pl.when((has == 1) & (other != row))
        def _():
            pltpu.make_async_copy(mf.at[other], mf.at[other], mrecv.at[other]).wait()
            split_factor(other)
            def body(t, carry):
                part_of = pl.ds(pl.multiple_of(t * BLOCK, BLOCK), BLOCK)
                turned = split(source[:, part_of].T)
                outm[slot, part_of, :] = dot3(turned, (mhi[row], mlo[row]))
                return carry
            lax.fori_loop(0, SIDE, body, 0)

        for place, slots in plan.items():
            if len(slots) > slot and slots[slot][0] != place[0]:
                @at(place)
                def _(place=place, taker=slots[slot][0]):
                    product_copy(place[0], slot, taker).start()

        @pl.when(has == 1)
        def _():
            def body(t, carry):
                part_of = pl.ds(pl.multiple_of(t * BLOCK, BLOCK), BLOCK)
                straight = split(source[part_of, :])
                acc[part_of, :] += dot3(straight, (mhi[other], mlo[other]))
                return carry
            lax.fori_loop(0, SIDE, body, 0)

    work(0)
    for place, listed in sends.items():
        late = [(i, s) for i, s in enumerate(listed) if s[3]]
        if late:
            @at(place)
            def _(late=late):
                for chunk in range(CHUNKS):
                    for index, (source_slot, target, slot, _) in late:
                        block_copy(index, source_slot, target, slot, chunk).start()
    relay(range(CHUNKS // 2, CHUNKS))
    for slot in range(1, SIDE):
        work(slot)

    for sender in range(SIDE):
        gets = lookup(me, {
            p: 1 for p in plan
            if p[0] != sender and any(s[0] == p[0] for s in plan[sender, p[1]])
        })

        @pl.when(gets == 1)
        def _(sender=sender):
            pltpu.make_async_copy(outm.at[0], pin.at[sender], precv.at[sender]).wait()
            acc[...] += pin[sender]

    def kept(value, level):
        return jnp.concatenate(
            [-(value[i * BLOCK:(i + 1) * BLOCK, :] * keep[level][i]) for i in range(SIDE)], axis=0
        )

    factors = (mhi[row], mlo[row])
    links = [split(anc_ref[0, i]) for i in range(3)]
    first = kept(acc[:, 0:BLOCK], 0)
    first_ref[...] = first
    first_split = split(first)
    inner_first = dot3(split(first.T), factors)
    part[0, 0] = inner_first[:, 0:BLOCK].T
    part[0, 1] = inner_first[:, BLOCK:2 * BLOCK]
    part[0, 2] = inner_first[:, 2 * BLOCK:]
    second = kept(acc[:, BLOCK:2 * BLOCK] + dot3(first_split, links[0]), 1)
    second_out[...] = second
    later = (factors[0][:, BLOCK:], factors[1][:, BLOCK:])
    inner_second = dot3(split(second.T), later)
    part[1, 0] = inner_second[:, 0:BLOCK].T
    part[1, 1] = inner_second[:, BLOCK:]
    third = kept(
        acc[:, 2 * BLOCK:] + dot3(split(second), links[1]) + dot3(first_split, links[2]), 2
    )
    third_out[...] = third
    last = (factors[0][:, 2 * BLOCK:], factors[1][:, 2 * BLOCK:])
    part[1, 2] = dot3(split(third.T), last).T

    mine = lax.rem(row, 2)
    sibling = row + 1 - 2 * mine
    across = lax.rem(row + 2, SIDE)

    def exchange(source, target, index, partner):
        copy = pltpu.make_async_remote_copy(
            src_ref=source,
            dst_ref=target,
            send_sem=rsend.at[index],
            recv_sem=rrecv.at[index],
            device_id={"row": partner},
            device_id_type=MESH,
        )
        copy.start()
        return copy

    copy = exchange(part.at[1 - mine], got_core, 0, sibling)
    copy.wait()
    half_sum[...] = part[mine] + got_core[...]
    copy = exchange(half_sum, got_row, 1, across)
    copy.wait()
    total[mine] = half_sum[...] + got_row[...]
    copy = exchange(total.at[mine], total.at[mine], 2, sibling)
    copy.wait()

    turned = [split(anc_ref[0, i].T) for i in range(3)]
    diag_1 = dinv_ref[0, 0] - total[0, 0]
    diag_1s = split(diag_1)
    cross = -(total[0, 1] + dot3(diag_1s, links[0]))
    cross_s = split(cross)
    diag_2 = dinv_ref[1, 0] - total[1, 0] - dot3(turned[0], cross_s)
    near = -(total[1, 1] + dot3(split(diag_2), links[1]) + dot3(split(cross.T), links[2]))
    far = -(total[0, 2] + dot3(cross_s, links[1]) + dot3(diag_1s, links[2]))
    diag_3 = dinv_ref[2, 0] - total[1, 2] - dot3(turned[1], split(near)) - dot3(turned[2], split(far))
    ancestral_ref[0, 0] = cross
    ancestral_ref[0, 1] = near
    ancestral_ref[0, 2] = far
    diagonal_ref[0, 0] = diag_1
    diagonal_ref[1, 0] = diag_2
    diagonal_ref[2, 0] = diag_3

    for place, listed in sends.items():
        @at(place)
        def _(place=place, listed=listed):
            for index, (source_slot, target, slot, _) in enumerate(listed):
                for chunk in range(CHUNKS):
                    block_copy(index, source_slot, target, slot, chunk).wait_send()
            for _, taker in needs[place]:
                factor_copy(place[0], taker).wait_send()
            for slot, (other, _, _) in enumerate(plan[place]):
                if other != place[0]:
                    product_copy(place[0], slot, other).wait_send()


def on_device_fused(
    known_inverse, lower_first, lower_second, lower_third, ancestor, diag_inverse,
    structure, pick_second, pick_third,
):
    rows = SIDE * BLOCK
    wide = 3 * BLOCK
    f32 = jnp.float32
    most = max(len(listed) for listed in transfers()[1].values())
    smem = pl.BlockSpec(memory_space=pltpu.SMEM)
    vmem = pl.BlockSpec(memory_space=pltpu.VMEM)
    dma = pltpu.SemaphoreType.DMA
    return pl.pallas_call(
        fused_kernel,
        out_shape=(
            jax.ShapeDtypeStruct((rows, BLOCK), f32),
            jax.ShapeDtypeStruct((rows, BLOCK), f32),
            jax.ShapeDtypeStruct((rows, BLOCK), f32),
            jax.ShapeDtypeStruct((1, 3, BLOCK, BLOCK), f32),
            jax.ShapeDtypeStruct((3, 1, BLOCK, BLOCK), f32),
        ),
        in_specs=[smem] * 3 + [vmem] * 6,
        out_specs=[vmem] * 5,
        scratch_shapes=[
            pltpu.VMEM((SIDE - 1, rows, rows), f32),
            pltpu.VMEM((SIDE, rows, wide), f32),
            pltpu.VMEM((SIDE, rows, wide), jnp.bfloat16),
            pltpu.VMEM((SIDE, rows, wide), jnp.bfloat16),
            pltpu.VMEM((rows, wide), f32),
            pltpu.VMEM((SIDE, rows, wide), f32),
            pltpu.VMEM((SIDE, rows, wide), f32),
            pltpu.VMEM((2, 3, BLOCK, BLOCK), f32),
            pltpu.VMEM((3, BLOCK, BLOCK), f32),
            pltpu.VMEM((3, BLOCK, BLOCK), f32),
            pltpu.VMEM((3, BLOCK, BLOCK), f32),
            pltpu.VMEM((2, 3, BLOCK, BLOCK), f32),
            dma((most, CHUNKS)),
            dma((SIDE - 1, CHUNKS)),
            dma((SIDE,)),
            dma((SIDE,)),
            dma((SIDE,)),
            dma((SIDE,)),
            dma((3,)),
            dma((3,)),
        ],
        compiler_params=pltpu.CompilerParams(
            collective_id=0, has_side_effects=True, vmem_limit_bytes=40 * 1024 * 1024
        ),
    )(
        structure, pick_second, pick_third, known_inverse, lower_first, lower_second, lower_third,
        ancestor, diag_inverse,
    )


def solution(mesh):
    fused = mesh.shape["row"] == SIDE and mesh.shape["col"] == SIDE
    placed = (
        P(("pole", "row"), "col"),
        P(("pole", "row"), "col"),
        P(("pole", "row"), "col"),
        P(("pole", "row"), "col"),
        P(("pole", "col"), None, None, None),
        P("pole", "col", None, None),
        P(),
        P(),
        P(),
    )
    return jax.shard_map(
        on_device_fused if fused else on_device,
        mesh=mesh,
        in_specs=placed,
        out_specs=(
            P(("pole", "row"), "col"),
            P(("pole", "row"), "col"),
            P(("pole", "row"), "col"),
            P(("pole", "col"), None, None, None),
            P("pole", "col", None, None),
        ),
        check_vma=False,
    )
```

```python
import jax
import jax.numpy as jnp
from jax import lax
from jax.experimental import pallas as pl
from jax.experimental.pallas import tpu as pltpu
from jax.sharding import PartitionSpec as P

HIGHEST = lax.Precision.HIGHEST


def broadcast(array, axis, root):
    mine = lax.axis_index(axis) == root
    return lax.psum(jnp.where(mine, array, jnp.zeros_like(array)), axis)


def block_mask(members, block_count):
    block_ids = jnp.arange(block_count, dtype=jnp.int32)
    return jnp.sum((members[:, :, None] == block_ids[None, None, :]).astype(jnp.float32), axis=1)


def structure_masks(structure, pick_second, pick_third, block_count):
    second_ids = jnp.take_along_axis(structure, pick_second, axis=1)
    third_ids = jnp.take_along_axis(second_ids, pick_third, axis=1)
    return (
        block_mask(structure, block_count),
        block_mask(second_ids, block_count),
        block_mask(third_ids, block_count),
    )


def expand_mask(mask_table, block_size):
    return jnp.repeat(jnp.repeat(mask_table.T, block_size, axis=0), block_size, axis=1)


def node_times(columns, blocks):
    height = columns.shape[0]
    node_count = blocks.shape[0]
    block_size = blocks.shape[1]
    reshaped = columns.reshape(height, node_count, block_size)
    return jnp.einsum("rkb,kbc->rkc", reshaped, blocks, precision=HIGHEST).reshape(
        height, node_count * block_size
    )


def node_inner(former, latter, block_size):
    height = former.shape[0]
    node_count = former.shape[1] // block_size
    return jnp.einsum(
        "rkb,rkc->kbc",
        former.reshape(height, node_count, block_size),
        latter.reshape(height, node_count, block_size),
        precision=HIGHEST,
    )


def block_product(former, latter):
    return jnp.einsum("kbc,kcd->kbd", former, latter, precision=HIGHEST)


def block_tproduct(former, latter):
    return jnp.einsum("kcb,kcd->kbd", former, latter, precision=HIGHEST)


def row_total(partial_sum):
    return lax.psum(partial_sum, "row")


def on_device(
    known_inverse,
    lower_first,
    lower_second,
    lower_third,
    ancestor,
    diag_inverse,
    structure,
    pick_second,
    pick_third,
):
    block_size = ancestor.shape[2]
    row_group = lax.axis_size("row") // lax.axis_size("col")
    local_blocks = known_inverse.shape[0] // block_size
    block_count = local_blocks * lax.axis_size("row")
    local_nodes = ancestor.shape[0]
    masks = structure_masks(structure, pick_second, pick_third, block_count)
    block_start = lax.axis_index("row") * local_blocks
    node_start = lax.axis_index("col") * local_nodes
    expanded = [
        expand_mask(
            lax.dynamic_slice(mask_table, (node_start, block_start), (local_nodes, local_blocks)),
            block_size,
        )
        for mask_table in masks
    ]
    lowers = [
        factor * kept_rows
        for factor, kept_rows in zip((lower_first, lower_second, lower_third), expanded)
    ]
    products = []
    for masked in lowers:
        gathered = lax.all_gather(masked, "col", axis=1, tiled=True)
        pieces = [
            broadcast(gathered, "row", lax.axis_index("col") * row_group + offset)
            for offset in range(row_group)
        ]
        partial_value = jnp.dot(known_inverse, jnp.concatenate(pieces, axis=0), precision=HIGHEST)
        products.append(lax.psum_scatter(partial_value, "col", scatter_dimension=1, tiled=True))
    link_two = ancestor[:, 0]
    link_near = ancestor[:, 1]
    link_far = ancestor[:, 2]
    first_cols = -expanded[0] * products[0]
    diag_first = diag_inverse[0] - row_total(node_inner(lowers[0], first_cols, block_size))
    second_cols = -expanded[1] * (products[1] + node_times(first_cols, link_two))
    parent_part = lax.psum(node_inner(first_cols, lowers[1], block_size), "row")
    cross_two = -(parent_part + block_product(diag_first, link_two))
    diag_second = (
        diag_inverse[1]
        - row_total(node_inner(lowers[1], second_cols, block_size))
        - block_tproduct(link_two, cross_two)
    )
    third_cols = -expanded[2] * (
        products[2] + node_times(second_cols, link_near) + node_times(first_cols, link_far)
    )
    near_part, far_part = lax.psum(
        (
            node_inner(second_cols, lowers[2], block_size),
            node_inner(first_cols, lowers[2], block_size),
        ),
        "row",
    )
    cross_near = -(
        near_part + block_product(diag_second, link_near) + block_tproduct(cross_two, link_far)
    )
    cross_far = -(
        far_part + block_product(cross_two, link_near) + block_product(diag_first, link_far)
    )
    diag_third = (
        diag_inverse[2]
        - row_total(node_inner(lowers[2], third_cols, block_size))
        - block_tproduct(link_near, cross_near)
        - block_tproduct(link_far, cross_far)
    )
    ancestral = jnp.stack([cross_two, cross_near, cross_far], axis=1)
    diagonal = jnp.stack([diag_first, diag_second, diag_third], axis=0)
    return (first_cols, second_cols, third_cols, ancestral, diagonal)


SIDE = 4
BLOCK = 128
CHUNKS = 8
MESH = pl.DeviceIdType.MESH


def landing_plan():
    half = {
        (0, 0): [],
        (1, 0): [(2, 2, False), (3, 3, True), (1, 1, True)],
        (2, 0): [(2, 1, False)],
        (3, 0): [(2, 1, False), (3, 1, False)],
        (0, 1): [(0, 0, False)],
        (1, 1): [],
        (2, 1): [(0, 0, False), (2, 2, False)],
        (3, 1): [(0, 0, False), (2, 2, False), (3, 3, False)],
    }
    plan = {}
    for (row, col), slots in half.items():
        plan[row, col] = [(col, None, False)] + slots
        plan[3 - row, 3 - col] = [(3 - col, None, False)] + [
            (3 - other, 3 - source, late) for other, source, late in slots
        ]
    return plan


def transfers():
    plan = landing_plan()
    sends = {place: [] for place in plan}
    for (row, col), slots in plan.items():
        for slot, (other, source, late) in enumerate(slots):
            if slot == 0:
                continue
            held = [have[0] for have in plan[row, source]]
            assert other in held
            sends[row, source].append((held.index(other), (row, col), slot, late))
    return plan, sends


def lookup(me, values):
    total = jnp.int32(0)
    for place, value in values.items():
        if value:
            total = total + jnp.where(me == place[0] * SIDE + place[1], jnp.int32(value), jnp.int32(0))
    return total


def split(value):
    high = value.astype(jnp.bfloat16)
    low = (value - high.astype(jnp.float32)).astype(jnp.bfloat16)
    return high, low


def mul(a, b):
    return jnp.dot(a, b, preferred_element_type=jnp.float32)


def dot3(left, right):
    return mul(left[0], right[0]) + (mul(left[0], right[1]) + mul(left[1], right[0]))


def fused_kernel(
    structure_in, second_in, third_in, k_ref, l1_in, l2_in, l3_in, anc_in, dinv_in,
    first_ref, second_out, third_out, ancestral_ref, diagonal_ref,
    structure_ref, second_ref, third_ref, lbuf, anc_ref, dinv_ref, copied,
    kbuf, mf, mhi, mlo, acc, outm, pin, part, got_core, half_sum, got_row, total,
    ksend, krecv, msend, mrecv, psend, precv, rsend, rrecv,
):
    row = lax.axis_index("row")
    col = lax.axis_index("col")
    me = row * SIDE + col
    plan, sends = transfers()
    rows_of = SIDE * BLOCK
    step_rows = rows_of // CHUNKS

    def at(place):
        return pl.when(me == place[0] * SIDE + place[1])

    def block_copy(index, source_slot, target, slot, chunk):
        rows = pl.ds(chunk * step_rows, step_rows)
        source = k_ref.at[rows] if source_slot == 0 else kbuf.at[source_slot, rows]
        return pltpu.make_async_remote_copy(
            src_ref=source,
            dst_ref=kbuf.at[slot, rows],
            send_sem=ksend.at[index, chunk],
            recv_sem=krecv.at[slot - 1, chunk],
            device_id={"col": target[1]},
            device_id_type=MESH,
        )

    def wait_block(slot, chunk):
        rows = pl.ds(chunk * step_rows, step_rows)
        pltpu.make_async_copy(k_ref.at[rows], kbuf.at[slot, rows], krecv.at[slot - 1, chunk]).wait()

    def factor_copy(owner, taker):
        return pltpu.make_async_remote_copy(
            src_ref=mf.at[owner],
            dst_ref=mf.at[owner],
            send_sem=msend.at[taker],
            recv_sem=mrecv.at[owner],
            device_id={"row": taker},
            device_id_type=MESH,
        )

    def product_copy(sender, slot, taker):
        return pltpu.make_async_remote_copy(
            src_ref=outm.at[slot],
            dst_ref=pin.at[sender],
            send_sem=psend.at[slot],
            recv_sem=precv.at[sender],
            device_id={"row": taker},
            device_id_type=MESH,
        )

    local = [
        pltpu.make_async_copy(source, target, copied.at[index])
        for index, (source, target) in enumerate([
            (structure_in, structure_ref), (second_in, second_ref), (third_in, third_ref),
            (l1_in, lbuf.at[0]), (l2_in, lbuf.at[1]), (l3_in, lbuf.at[2]),
            (k_ref, kbuf.at[0]), (anc_in, anc_ref), (dinv_in, dinv_ref),
        ])
    ]
    for copy in local:
        copy.start()

    barrier = pltpu.get_barrier_semaphore()
    for step in range(1, SIDE):
        pl.semaphore_signal(barrier, inc=1, device_id={"col": lax.rem(col + step, SIDE)}, device_id_type=MESH)
        pl.semaphore_signal(barrier, inc=1, device_id={"row": lax.rem(row + step, SIDE)}, device_id_type=MESH)
    pl.semaphore_wait(barrier, 2 * (SIDE - 1))

    for place, listed in sends.items():
        early = [(i, s) for i, s in enumerate(listed) if s[0] == 0 and not s[3]]
        if early:
            @at(place)
            def _(early=early):
                for chunk in range(CHUNKS):
                    for index, (source_slot, target, slot, _) in early:
                        block_copy(index, source_slot, target, slot, chunk).start()

    for copy in local[:6]:
        copy.wait()

    def marks(ids, block):
        total_mark = jnp.float32(0)
        for one in ids:
            total_mark = total_mark + jnp.where(one == block, jnp.float32(1), jnp.float32(0))
        return total_mark

    ids_1 = [structure_ref[col, i] for i in range(structure_ref.shape[1])]
    ids_2 = [structure_ref[col, second_ref[col, i]] for i in range(second_ref.shape[1])]
    ids_3 = [
        structure_ref[col, second_ref[col, third_ref[col, i]]] for i in range(third_ref.shape[1])
    ]
    keep = [[marks(ids, row * SIDE + i) for i in range(SIDE)] for ids in (ids_1, ids_2, ids_3)]
    for level in range(3):
        for i in range(SIDE):
            rows = slice(i * BLOCK, (i + 1) * BLOCK)
            columns = slice(level * BLOCK, (level + 1) * BLOCK)
            mf[row, rows, columns] = lbuf[level, rows, :] * keep[level][i]

    needs = {place: [] for place in plan}
    for (r, k), slots in plan.items():
        for slot, (other, _, _) in enumerate(slots):
            if other != r:
                needs[other, k].append((slot, r))
    for (b, k), takers in needs.items():
        if takers:
            @at((b, k))
            def _(b=b, takers=takers):
                for _, taker in sorted(takers):
                    factor_copy(b, taker).start()

    acc[...] = jnp.zeros_like(acc)

    def split_factor(index):
        def body(t, carry):
            rows = pl.ds(pl.multiple_of(t * BLOCK, BLOCK), BLOCK)
            high, low = split(mf[index, rows, :])
            mhi[index, rows, :] = high
            mlo[index, rows, :] = low
            return carry
        lax.fori_loop(0, SIDE, body, 0)

    split_factor(row)

    def relay(chunks):
        for place, listed in sends.items():
            passed = [(i, s) for i, s in enumerate(listed) if s[0] != 0]
            if passed:
                @at(place)
                def _(passed=passed):
                    for chunk in chunks:
                        for index, (source_slot, target, slot, _) in passed:
                            wait_block(source_slot, chunk)
                            block_copy(index, source_slot, target, slot, chunk).start()

    for copy in local[6:]:
        copy.wait()

    has_slot = [lookup(me, {p: int(len(s) > slot) for p, s in plan.items()}) for slot in range(SIDE)]
    other_of = [
        lookup(me, {p: s[slot][0] for p, s in plan.items() if len(s) > slot}) for slot in range(SIDE)
    ]

    def arrive(slot):
        relayed = {p: int(any(s[0] == slot for s in listed)) for p, listed in sends.items()}
        fresh = has_slot[slot] - lookup(me, relayed)

        @pl.when(fresh == 1)
        def _():
            for chunk in range(CHUNKS):
                wait_block(slot, chunk)

    def message(slot):
        @pl.when((has_slot[slot] == 1) & (other_of[slot] != row))
        def _():
            def body(t, carry):
                part_of = pl.ds(pl.multiple_of(t * BLOCK, BLOCK), BLOCK)
                turned = split(kbuf[slot, :, part_of].T)
                outm[slot, part_of, :] = dot3(turned, (mhi[row], mlo[row]))
                return carry
            lax.fori_loop(0, SIDE, body, 0)

        for place, slots in plan.items():
            if len(slots) > slot and slots[slot][0] != place[0]:
                @at(place)
                def _(place=place, taker=slots[slot][0]):
                    product_copy(place[0], slot, taker).start()

    def collect(slot):
        other = other_of[slot]

        @pl.when((has_slot[slot] == 1) & (other != row))
        def _():
            pltpu.make_async_copy(mf.at[other], mf.at[other], mrecv.at[other]).wait()
            split_factor(other)

        @pl.when(has_slot[slot] == 1)
        def _():
            def body(t, carry):
                part_of = pl.ds(pl.multiple_of(t * BLOCK, BLOCK), BLOCK)
                straight = split(kbuf[slot, part_of, :])
                acc[part_of, :] += dot3(straight, (mhi[other], mlo[other]))
                return carry
            lax.fori_loop(0, SIDE, body, 0)

    message(0)
    relay(range(0, 3))
    collect(0)
    for place, listed in sends.items():
        late = [(i, s) for i, s in enumerate(listed) if s[3]]
        if late:
            @at(place)
            def _(late=late):
                for chunk in range(CHUNKS):
                    for index, (source_slot, target, slot, _) in late:
                        block_copy(index, source_slot, target, slot, chunk).start()
    arrive(1)
    message(1)
    relay(range(3, 6))
    collect(1)
    relay(range(6, CHUNKS))
    arrive(2)
    message(2)
    collect(2)
    arrive(3)
    message(3)
    collect(3)

    for sender in range(SIDE):
        gets = lookup(me, {
            p: 1 for p in plan
            if p[0] != sender and any(s[0] == p[0] for s in plan[sender, p[1]])
        })

        @pl.when(gets == 1)
        def _(sender=sender):
            pltpu.make_async_copy(outm.at[0], pin.at[sender], precv.at[sender]).wait()
            acc[...] += pin[sender]

    def kept(value, level):
        return jnp.concatenate(
            [-(value[i * BLOCK:(i + 1) * BLOCK, :] * keep[level][i]) for i in range(SIDE)], axis=0
        )

    factors = (mhi[row], mlo[row])
    links = [split(anc_ref[0, i]) for i in range(3)]
    first = kept(acc[:, 0:BLOCK], 0)
    first_ref[...] = first
    first_split = split(first)
    inner_first = dot3(split(first.T), factors)
    part[0, 0] = inner_first[:, 0:BLOCK].T
    part[0, 1] = inner_first[:, BLOCK:2 * BLOCK]
    part[0, 2] = inner_first[:, 2 * BLOCK:]
    second = kept(acc[:, BLOCK:2 * BLOCK] + dot3(first_split, links[0]), 1)
    second_out[...] = second
    later = (factors[0][:, BLOCK:], factors[1][:, BLOCK:])
    inner_second = dot3(split(second.T), later)
    part[1, 0] = inner_second[:, 0:BLOCK].T
    part[1, 1] = inner_second[:, BLOCK:]
    third = kept(
        acc[:, 2 * BLOCK:] + dot3(split(second), links[1]) + dot3(first_split, links[2]), 2
    )
    third_out[...] = third
    last = (factors[0][:, 2 * BLOCK:], factors[1][:, 2 * BLOCK:])
    part[1, 2] = dot3(split(third.T), last).T

    mine = lax.rem(row, 2)
    sibling = row + 1 - 2 * mine
    across = lax.rem(row + 2, SIDE)

    def exchange(source, target, index, partner):
        copy = pltpu.make_async_remote_copy(
            src_ref=source,
            dst_ref=target,
            send_sem=rsend.at[index],
            recv_sem=rrecv.at[index],
            device_id={"row": partner},
            device_id_type=MESH,
        )
        copy.start()
        return copy

    copy = exchange(part.at[1 - mine], got_core, 0, sibling)
    copy.wait()
    half_sum[...] = part[mine] + got_core[...]
    copy = exchange(half_sum, got_row, 1, across)
    copy.wait()
    total[mine] = half_sum[...] + got_row[...]
    copy = exchange(total.at[mine], total.at[mine], 2, sibling)
    copy.wait()

    turned = [split(anc_ref[0, i].T) for i in range(3)]
    diag_1 = dinv_ref[0, 0] - total[0, 0]
    diag_1s = split(diag_1)
    cross = -(total[0, 1] + dot3(diag_1s, links[0]))
    cross_s = split(cross)
    diag_2 = dinv_ref[1, 0] - total[1, 0] - dot3(turned[0], cross_s)
    near = -(total[1, 1] + dot3(split(diag_2), links[1]) + dot3(split(cross.T), links[2]))
    far = -(total[0, 2] + dot3(cross_s, links[1]) + dot3(diag_1s, links[2]))
    diag_3 = dinv_ref[2, 0] - total[1, 2] - dot3(turned[1], split(near)) - dot3(turned[2], split(far))
    ancestral_ref[0, 0] = cross
    ancestral_ref[0, 1] = near
    ancestral_ref[0, 2] = far
    diagonal_ref[0, 0] = diag_1
    diagonal_ref[1, 0] = diag_2
    diagonal_ref[2, 0] = diag_3

    for place, listed in sends.items():
        @at(place)
        def _(place=place, listed=listed):
            for index, (source_slot, target, slot, _) in enumerate(listed):
                for chunk in range(CHUNKS):
                    block_copy(index, source_slot, target, slot, chunk).wait_send()
            for _, taker in needs[place]:
                factor_copy(place[0], taker).wait_send()
            for slot, (other, _, _) in enumerate(plan[place]):
                if other != place[0]:
                    product_copy(place[0], slot, other).wait_send()


def on_device_fused(
    known_inverse, lower_first, lower_second, lower_third, ancestor, diag_inverse,
    structure, pick_second, pick_third,
):
    rows = SIDE * BLOCK
    wide = 3 * BLOCK
    f32 = jnp.float32
    most = max(len(listed) for listed in transfers()[1].values())
    vmem = pl.BlockSpec(memory_space=pltpu.VMEM)
    dma = pltpu.SemaphoreType.DMA
    return pl.pallas_call(
        fused_kernel,
        out_shape=(
            jax.ShapeDtypeStruct((rows, BLOCK), f32),
            jax.ShapeDtypeStruct((rows, BLOCK), f32),
            jax.ShapeDtypeStruct((rows, BLOCK), f32),
            jax.ShapeDtypeStruct((1, 3, BLOCK, BLOCK), f32),
            jax.ShapeDtypeStruct((3, 1, BLOCK, BLOCK), f32),
        ),
        in_specs=[pl.BlockSpec(memory_space=pl.ANY)] * 9,
        out_specs=[vmem] * 5,
        scratch_shapes=[
            pltpu.SMEM(structure.shape, jnp.int32),
            pltpu.SMEM(pick_second.shape, jnp.int32),
            pltpu.SMEM(pick_third.shape, jnp.int32),
            pltpu.VMEM((3, rows, BLOCK), f32),
            pltpu.VMEM(ancestor.shape, f32),
            pltpu.VMEM(diag_inverse.shape, f32),
            dma((9,)),
            pltpu.VMEM((SIDE, rows, rows), f32),
            pltpu.VMEM((SIDE, rows, wide), f32),
            pltpu.VMEM((SIDE, rows, wide), jnp.bfloat16),
            pltpu.VMEM((SIDE, rows, wide), jnp.bfloat16),
            pltpu.VMEM((rows, wide), f32),
            pltpu.VMEM((SIDE, rows, wide), f32),
            pltpu.VMEM((SIDE, rows, wide), f32),
            pltpu.VMEM((2, 3, BLOCK, BLOCK), f32),
            pltpu.VMEM((3, BLOCK, BLOCK), f32),
            pltpu.VMEM((3, BLOCK, BLOCK), f32),
            pltpu.VMEM((3, BLOCK, BLOCK), f32),
            pltpu.VMEM((2, 3, BLOCK, BLOCK), f32),
            dma((most, CHUNKS)),
            dma((SIDE - 1, CHUNKS)),
            dma((SIDE,)),
            dma((SIDE,)),
            dma((SIDE,)),
            dma((SIDE,)),
            dma((3,)),
            dma((3,)),
        ],
        compiler_params=pltpu.CompilerParams(
            collective_id=0, has_side_effects=True, vmem_limit_bytes=60 * 1024 * 1024
        ),
    )(
        structure, pick_second, pick_third, known_inverse, lower_first, lower_second, lower_third,
        ancestor, diag_inverse,
    )


def solution(mesh):
    fused = mesh.shape["row"] == SIDE and mesh.shape["col"] == SIDE
    placed = (
        P(("pole", "row"), "col"),
        P(("pole", "row"), "col"),
        P(("pole", "row"), "col"),
        P(("pole", "row"), "col"),
        P(("pole", "col"), None, None, None),
        P("pole", "col", None, None),
        P(),
        P(),
        P(),
    )
    return jax.shard_map(
        on_device_fused if fused else on_device,
        mesh=mesh,
        in_specs=placed,
        out_specs=(
            P(("pole", "row"), "col"),
            P(("pole", "row"), "col"),
            P(("pole", "row"), "col"),
            P(("pole", "col"), None, None, None),
            P("pole", "col", None, None),
        ),
        check_vma=False,
    )
```

```python
import jax
import jax.numpy as jnp
from jax import lax
from jax.experimental import pallas as pl
from jax.experimental.pallas import tpu as pltpu
from jax.sharding import PartitionSpec as P

HIGHEST = lax.Precision.HIGHEST


def broadcast(array, axis, root):
    mine = lax.axis_index(axis) == root
    return lax.psum(jnp.where(mine, array, jnp.zeros_like(array)), axis)


def block_mask(members, block_count):
    block_ids = jnp.arange(block_count, dtype=jnp.int32)
    return jnp.sum((members[:, :, None] == block_ids[None, None, :]).astype(jnp.float32), axis=1)


def structure_masks(structure, pick_second, pick_third, block_count):
    second_ids = jnp.take_along_axis(structure, pick_second, axis=1)
    third_ids = jnp.take_along_axis(second_ids, pick_third, axis=1)
    return (
        block_mask(structure, block_count),
        block_mask(second_ids, block_count),
        block_mask(third_ids, block_count),
    )


def expand_mask(mask_table, block_size):
    return jnp.repeat(jnp.repeat(mask_table.T, block_size, axis=0), block_size, axis=1)


def node_times(columns, blocks):
    height = columns.shape[0]
    node_count = blocks.shape[0]
    block_size = blocks.shape[1]
    reshaped = columns.reshape(height, node_count, block_size)
    return jnp.einsum("rkb,kbc->rkc", reshaped, blocks, precision=HIGHEST).reshape(
        height, node_count * block_size
    )


def node_inner(former, latter, block_size):
    height = former.shape[0]
    node_count = former.shape[1] // block_size
    return jnp.einsum(
        "rkb,rkc->kbc",
        former.reshape(height, node_count, block_size),
        latter.reshape(height, node_count, block_size),
        precision=HIGHEST,
    )


def block_product(former, latter):
    return jnp.einsum("kbc,kcd->kbd", former, latter, precision=HIGHEST)


def block_tproduct(former, latter):
    return jnp.einsum("kcb,kcd->kbd", former, latter, precision=HIGHEST)


def row_total(partial_sum):
    return lax.psum(partial_sum, "row")


def on_device(
    known_inverse,
    lower_first,
    lower_second,
    lower_third,
    ancestor,
    diag_inverse,
    structure,
    pick_second,
    pick_third,
):
    block_size = ancestor.shape[2]
    row_group = lax.axis_size("row") // lax.axis_size("col")
    local_blocks = known_inverse.shape[0] // block_size
    block_count = local_blocks * lax.axis_size("row")
    local_nodes = ancestor.shape[0]
    masks = structure_masks(structure, pick_second, pick_third, block_count)
    block_start = lax.axis_index("row") * local_blocks
    node_start = lax.axis_index("col") * local_nodes
    expanded = [
        expand_mask(
            lax.dynamic_slice(mask_table, (node_start, block_start), (local_nodes, local_blocks)),
            block_size,
        )
        for mask_table in masks
    ]
    lowers = [
        factor * kept_rows
        for factor, kept_rows in zip((lower_first, lower_second, lower_third), expanded)
    ]
    products = []
    for masked in lowers:
        gathered = lax.all_gather(masked, "col", axis=1, tiled=True)
        pieces = [
            broadcast(gathered, "row", lax.axis_index("col") * row_group + offset)
            for offset in range(row_group)
        ]
        partial_value = jnp.dot(known_inverse, jnp.concatenate(pieces, axis=0), precision=HIGHEST)
        products.append(lax.psum_scatter(partial_value, "col", scatter_dimension=1, tiled=True))
    link_two = ancestor[:, 0]
    link_near = ancestor[:, 1]
    link_far = ancestor[:, 2]
    first_cols = -expanded[0] * products[0]
    diag_first = diag_inverse[0] - row_total(node_inner(lowers[0], first_cols, block_size))
    second_cols = -expanded[1] * (products[1] + node_times(first_cols, link_two))
    parent_part = lax.psum(node_inner(first_cols, lowers[1], block_size), "row")
    cross_two = -(parent_part + block_product(diag_first, link_two))
    diag_second = (
        diag_inverse[1]
        - row_total(node_inner(lowers[1], second_cols, block_size))
        - block_tproduct(link_two, cross_two)
    )
    third_cols = -expanded[2] * (
        products[2] + node_times(second_cols, link_near) + node_times(first_cols, link_far)
    )
    near_part, far_part = lax.psum(
        (
            node_inner(second_cols, lowers[2], block_size),
            node_inner(first_cols, lowers[2], block_size),
        ),
        "row",
    )
    cross_near = -(
        near_part + block_product(diag_second, link_near) + block_tproduct(cross_two, link_far)
    )
    cross_far = -(
        far_part + block_product(cross_two, link_near) + block_product(diag_first, link_far)
    )
    diag_third = (
        diag_inverse[2]
        - row_total(node_inner(lowers[2], third_cols, block_size))
        - block_tproduct(link_near, cross_near)
        - block_tproduct(link_far, cross_far)
    )
    ancestral = jnp.stack([cross_two, cross_near, cross_far], axis=1)
    diagonal = jnp.stack([diag_first, diag_second, diag_third], axis=0)
    return (first_cols, second_cols, third_cols, ancestral, diagonal)


SIDE = 4
BLOCK = 128
CHUNKS = 8
MESH = pl.DeviceIdType.MESH


def landing_plan():
    half = {
        (0, 0): [],
        (1, 0): [(2, 2, False), (3, 2, False), (1, 1, True)],
        (2, 0): [(2, 1, False)],
        (3, 0): [(2, 1, False), (3, 1, False)],
        (0, 1): [(0, 0, False)],
        (1, 1): [],
        (2, 1): [(0, 0, False), (2, 2, False)],
        (3, 1): [(0, 0, False), (2, 2, False), (3, 3, False)],
    }
    plan = {}
    for (row, col), slots in half.items():
        plan[row, col] = [(col, None, False)] + slots
        plan[3 - row, 3 - col] = [(3 - col, None, False)] + [
            (3 - other, 3 - source, late) for other, source, late in slots
        ]
    return plan


def transfers():
    plan = landing_plan()
    sends = {place: [] for place in plan}
    for (row, col), slots in plan.items():
        for slot, (other, source, late) in enumerate(slots):
            if slot == 0:
                continue
            held = [have[0] for have in plan[row, source]]
            assert other in held
            sends[row, source].append((held.index(other), (row, col), slot, late))
    return plan, sends


FOLDS = {(3, 1): 2, (0, 2): 1}


def product_sends(plan):
    return {
        (place, slot): entry[0]
        for place, slots in plan.items()
        for slot, entry in enumerate(slots)
        if entry[0] != place[0] and not (place in FOLDS and slot == 1)
    }


def factor_sends(plan):
    direct = {place: [] for place in plan}
    passes = {}
    for owner, col in plan:
        takers = [
            row for row in range(SIDE)
            if row != owner and any(entry[0] == owner for entry in plan[row, col])
        ]
        near = (owner + 2) % SIDE
        far = near + 1 - 2 * (near % 2)
        if near in takers and far in takers:
            takers.remove(far)
            assert (near, col) not in passes
            passes[near, col] = (owner, far)
        direct[owner, col] = takers
    return direct, passes


def lookup(me, values):
    total = jnp.int32(0)
    for place, value in values.items():
        if value:
            total = total + jnp.where(me == place[0] * SIDE + place[1], jnp.int32(value), jnp.int32(0))
    return total


def split(value):
    high = value.astype(jnp.bfloat16)
    low = (value - high.astype(jnp.float32)).astype(jnp.bfloat16)
    return high, low


def mul(a, b):
    return jnp.dot(a, b, preferred_element_type=jnp.float32)


def dot3(left, right):
    return mul(left[0], right[0]) + (mul(left[0], right[1]) + mul(left[1], right[0]))


def fused_kernel(
    structure_in, second_in, third_in, k_ref, l1_in, l2_in, l3_in, anc_in, dinv_in,
    first_ref, second_out, third_out, ancestral_ref, diagonal_ref,
    structure_ref, second_ref, third_ref, lbuf, anc_ref, dinv_ref, copied,
    kbuf, mf, mhi, mlo, acc, outm, pin, fold, part, got_core, half_sum, got_row, total,
    ksend, krecv, msend, mrecv, psend, precv, fsem, rsend, rrecv,
):
    row = lax.axis_index("row")
    col = lax.axis_index("col")
    me = row * SIDE + col
    plan, sends = transfers()
    rows_of = SIDE * BLOCK
    step_rows = rows_of // CHUNKS

    def at(place):
        return pl.when(me == place[0] * SIDE + place[1])

    def block_copy(index, source_slot, target, slot, chunk):
        rows = pl.ds(chunk * step_rows, step_rows)
        source = k_ref.at[rows] if source_slot == 0 else kbuf.at[source_slot, rows]
        return pltpu.make_async_remote_copy(
            src_ref=source,
            dst_ref=kbuf.at[slot, rows],
            send_sem=ksend.at[index, chunk],
            recv_sem=krecv.at[slot - 1, chunk],
            device_id={"col": target[1]},
            device_id_type=MESH,
        )

    def wait_block(slot, chunk):
        rows = pl.ds(chunk * step_rows, step_rows)
        pltpu.make_async_copy(k_ref.at[rows], kbuf.at[slot, rows], krecv.at[slot - 1, chunk]).wait()

    def fold_copy(taker):
        return pltpu.make_async_remote_copy(
            src_ref=outm.at[1],
            dst_ref=fold,
            send_sem=psend.at[1],
            recv_sem=fsem,
            device_id={"row": taker},
            device_id_type=MESH,
        )

    def wait_factor(owner):
        pltpu.make_async_copy(mf.at[owner], mf.at[owner], mrecv.at[owner]).wait()

    def factor_copy(owner, taker):
        return pltpu.make_async_remote_copy(
            src_ref=mf.at[owner],
            dst_ref=mf.at[owner],
            send_sem=msend.at[taker],
            recv_sem=mrecv.at[owner],
            device_id={"row": taker},
            device_id_type=MESH,
        )

    def product_copy(sender, slot, taker):
        return pltpu.make_async_remote_copy(
            src_ref=outm.at[slot],
            dst_ref=pin.at[sender],
            send_sem=psend.at[slot],
            recv_sem=precv.at[sender],
            device_id={"row": taker},
            device_id_type=MESH,
        )

    local = [
        pltpu.make_async_copy(source, target, copied.at[index])
        for index, (source, target) in enumerate([
            (structure_in, structure_ref), (second_in, second_ref), (third_in, third_ref),
            (l1_in, lbuf.at[0]), (l2_in, lbuf.at[1]), (l3_in, lbuf.at[2]),
            (k_ref, kbuf.at[0]), (anc_in, anc_ref), (dinv_in, dinv_ref),
        ])
    ]
    for copy in local:
        copy.start()

    barrier = pltpu.get_barrier_semaphore()
    for step in range(1, SIDE):
        pl.semaphore_signal(barrier, inc=1, device_id={"col": lax.rem(col + step, SIDE)}, device_id_type=MESH)
        pl.semaphore_signal(barrier, inc=1, device_id={"row": lax.rem(row + step, SIDE)}, device_id_type=MESH)
    pl.semaphore_wait(barrier, 2 * (SIDE - 1))

    for place, listed in sends.items():
        early = [(i, s) for i, s in enumerate(listed) if s[0] == 0 and not s[3]]
        if early:
            @at(place)
            def _(early=early):
                for chunk in range(CHUNKS):
                    for index, (source_slot, target, slot, _) in early:
                        block_copy(index, source_slot, target, slot, chunk).start()

    for copy in local[:6]:
        copy.wait()

    def marks(ids, block):
        total_mark = jnp.float32(0)
        for one in ids:
            total_mark = total_mark + jnp.where(one == block, jnp.float32(1), jnp.float32(0))
        return total_mark

    ids_1 = [structure_ref[col, i] for i in range(structure_ref.shape[1])]
    ids_2 = [structure_ref[col, second_ref[col, i]] for i in range(second_ref.shape[1])]
    ids_3 = [
        structure_ref[col, second_ref[col, third_ref[col, i]]] for i in range(third_ref.shape[1])
    ]
    keep = [[marks(ids, row * SIDE + i) for i in range(SIDE)] for ids in (ids_1, ids_2, ids_3)]
    for level in range(3):
        for i in range(SIDE):
            rows = slice(i * BLOCK, (i + 1) * BLOCK)
            columns = slice(level * BLOCK, (level + 1) * BLOCK)
            mf[row, rows, columns] = lbuf[level, rows, :] * keep[level][i]

    direct, passes = factor_sends(plan)
    products = product_sends(plan)
    for place, takers in direct.items():
        if takers:
            @at(place)
            def _(place=place, takers=takers):
                for taker in takers:
                    factor_copy(place[0], taker).start()

    acc[...] = jnp.zeros_like(acc)

    def split_factor(index):
        def body(t, carry):
            rows = pl.ds(pl.multiple_of(t * BLOCK, BLOCK), BLOCK)
            high, low = split(mf[index, rows, :])
            mhi[index, rows, :] = high
            mlo[index, rows, :] = low
            return carry
        lax.fori_loop(0, SIDE, body, 0)

    split_factor(row)

    def relay(chunks, slots_passed):
        for place, listed in sends.items():
            passed = [(i, s) for i, s in enumerate(listed) if s[0] in slots_passed]
            if passed:
                @at(place)
                def _(passed=passed):
                    for chunk in chunks:
                        for index, (source_slot, target, slot, _) in passed:
                            wait_block(source_slot, chunk)
                            block_copy(index, source_slot, target, slot, chunk).start()

    for copy in local[6:]:
        copy.wait()

    has_slot = [lookup(me, {p: int(len(s) > slot) for p, s in plan.items()}) for slot in range(SIDE)]
    other_of = [
        lookup(me, {p: s[slot][0] for p, s in plan.items() if len(s) > slot}) for slot in range(SIDE)
    ]

    def arrive(slot):
        relayed = {p: int(any(s[0] == slot for s in listed)) for p, listed in sends.items()}
        fresh = has_slot[slot] - lookup(me, relayed)

        @pl.when(fresh == 1)
        def _():
            for chunk in range(CHUNKS):
                wait_block(slot, chunk)

    def message(slot):
        @pl.when((has_slot[slot] == 1) & (other_of[slot] != row))
        def _():
            def body(t, carry):
                part_of = pl.ds(pl.multiple_of(t * BLOCK, BLOCK), BLOCK)
                turned = split(kbuf[slot, :, part_of].T)
                outm[slot, part_of, :] = dot3(turned, (mhi[row], mlo[row]))
                return carry
            lax.fori_loop(0, SIDE, body, 0)

        if slot == 1:
            for place, taker in FOLDS.items():
                @at(place)
                def _(taker=taker):
                    fold_copy(taker).start()

                @at((taker, place[1]))
                def _():
                    pltpu.make_async_copy(outm.at[1], fold, fsem).wait()
                    outm[1] += fold[...]

        for (place, at_slot), taker in products.items():
            if at_slot == slot:
                @at(place)
                def _(place=place, taker=taker):
                    product_copy(place[0], slot, taker).start()

    def collect(slot):
        other = other_of[slot]

        passed = lookup(me, {
            p: 1 for p, (owner, _) in passes.items()
            if len(plan[p]) > slot and plan[p][slot][0] == owner
        })

        @pl.when((has_slot[slot] == 1) & (other != row) & (passed == 0))
        def _():
            wait_factor(other)

        @pl.when((has_slot[slot] == 1) & (other != row))
        def _():
            split_factor(other)

        @pl.when(has_slot[slot] == 1)
        def _():
            def body(t, carry):
                part_of = pl.ds(pl.multiple_of(t * BLOCK, BLOCK), BLOCK)
                straight = split(kbuf[slot, part_of, :])
                acc[part_of, :] += dot3(straight, (mhi[other], mlo[other]))
                return carry
            lax.fori_loop(0, SIDE, body, 0)

    every = range(1, SIDE)
    message(0)
    relay(range(0, 3), every)
    for place, (owner, taker) in passes.items():
        @at(place)
        def _(owner=owner, taker=taker, place=place):
            wait_factor(owner)
            pltpu.make_async_remote_copy(
                src_ref=mf.at[owner],
                dst_ref=mf.at[owner],
                send_sem=msend.at[place[0]],
                recv_sem=mrecv.at[owner],
                device_id={"row": taker},
                device_id_type=MESH,
            ).start()
    relay(range(3, 4), every)
    collect(0)
    relay(range(4, 6), every)
    relay(range(6, CHUNKS), [1])
    arrive(1)
    message(1)
    relay(range(6, 7), [2, 3])
    collect(1)
    relay(range(7, CHUNKS), [2, 3])
    arrive(2)
    message(2)
    collect(2)
    arrive(3)
    message(3)
    collect(3)

    for sender in range(SIDE):
        gets = lookup(me, {
            p: 1 for p in plan
            if any(q == (sender, p[1]) and taker == p[0] for (q, _), taker in products.items())
        })

        @pl.when(gets == 1)
        def _(sender=sender):
            pltpu.make_async_copy(outm.at[0], pin.at[sender], precv.at[sender]).wait()
            acc[...] += pin[sender]

    for place, listed in sends.items():
        late = [(i, s) for i, s in enumerate(listed) if s[3]]
        if late:
            @at(place)
            def _(late=late):
                for chunk in range(CHUNKS):
                    for index, (source_slot, target, slot, _) in late:
                        block_copy(index, source_slot, target, slot, chunk).start()

    def kept(value, level):
        return jnp.concatenate(
            [-(value[i * BLOCK:(i + 1) * BLOCK, :] * keep[level][i]) for i in range(SIDE)], axis=0
        )

    factors = (mhi[row], mlo[row])
    links = [split(anc_ref[0, i]) for i in range(3)]
    first = kept(acc[:, 0:BLOCK], 0)
    first_ref[...] = first
    first_split = split(first)
    inner_first = dot3(split(first.T), factors)
    part[0, 0] = inner_first[:, 0:BLOCK].T
    part[0, 1] = inner_first[:, BLOCK:2 * BLOCK]
    part[0, 2] = inner_first[:, 2 * BLOCK:]
    second = kept(acc[:, BLOCK:2 * BLOCK] + dot3(first_split, links[0]), 1)
    second_out[...] = second
    later = (factors[0][:, BLOCK:], factors[1][:, BLOCK:])
    inner_second = dot3(split(second.T), later)
    part[1, 0] = inner_second[:, 0:BLOCK].T
    part[1, 1] = inner_second[:, BLOCK:]
    third = kept(
        acc[:, 2 * BLOCK:] + dot3(split(second), links[1]) + dot3(first_split, links[2]), 2
    )
    third_out[...] = third
    last = (factors[0][:, 2 * BLOCK:], factors[1][:, 2 * BLOCK:])
    part[1, 2] = dot3(split(third.T), last).T

    mine = lax.rem(row, 2)
    sibling = row + 1 - 2 * mine
    across = lax.rem(row + 2, SIDE)

    def exchange(source, target, index, partner):
        copy = pltpu.make_async_remote_copy(
            src_ref=source,
            dst_ref=target,
            send_sem=rsend.at[index],
            recv_sem=rrecv.at[index],
            device_id={"row": partner},
            device_id_type=MESH,
        )
        copy.start()
        return copy

    copy = exchange(part.at[1 - mine], got_core, 0, sibling)
    copy.wait()
    half_sum[...] = part[mine] + got_core[...]
    copy = exchange(half_sum, got_row, 1, across)
    copy.wait()
    total[mine] = half_sum[...] + got_row[...]
    copy = exchange(total.at[mine], total.at[mine], 2, sibling)
    copy.wait()

    turned = [split(anc_ref[0, i].T) for i in range(3)]
    diag_1 = dinv_ref[0, 0] - total[0, 0]
    diag_1s = split(diag_1)
    cross = -(total[0, 1] + dot3(diag_1s, links[0]))
    cross_s = split(cross)
    diag_2 = dinv_ref[1, 0] - total[1, 0] - dot3(turned[0], cross_s)
    near = -(total[1, 1] + dot3(split(diag_2), links[1]) + dot3(split(cross.T), links[2]))
    far = -(total[0, 2] + dot3(cross_s, links[1]) + dot3(diag_1s, links[2]))
    diag_3 = dinv_ref[2, 0] - total[1, 2] - dot3(turned[1], split(near)) - dot3(turned[2], split(far))
    ancestral_ref[0, 0] = cross
    ancestral_ref[0, 1] = near
    ancestral_ref[0, 2] = far
    diagonal_ref[0, 0] = diag_1
    diagonal_ref[1, 0] = diag_2
    diagonal_ref[2, 0] = diag_3

    for place, listed in sends.items():
        @at(place)
        def _(place=place, listed=listed):
            for index, (source_slot, target, slot, _) in enumerate(listed):
                for chunk in range(CHUNKS):
                    block_copy(index, source_slot, target, slot, chunk).wait_send()
            for taker in direct[place]:
                factor_copy(place[0], taker).wait_send()
            if place in passes:
                pltpu.make_async_copy(mf.at[0], mf.at[0], msend.at[place[0]]).wait()
            if place in FOLDS:
                fold_copy(FOLDS[place]).wait_send()
            for (origin, slot), taker in products.items():
                if origin == place:
                    product_copy(place[0], slot, taker).wait_send()


def on_device_fused(
    known_inverse, lower_first, lower_second, lower_third, ancestor, diag_inverse,
    structure, pick_second, pick_third,
):
    rows = SIDE * BLOCK
    wide = 3 * BLOCK
    f32 = jnp.float32
    most = max(len(listed) for listed in transfers()[1].values())
    vmem = pl.BlockSpec(memory_space=pltpu.VMEM)
    dma = pltpu.SemaphoreType.DMA
    return pl.pallas_call(
        fused_kernel,
        out_shape=(
            jax.ShapeDtypeStruct((rows, BLOCK), f32),
            jax.ShapeDtypeStruct((rows, BLOCK), f32),
            jax.ShapeDtypeStruct((rows, BLOCK), f32),
            jax.ShapeDtypeStruct((1, 3, BLOCK, BLOCK), f32),
            jax.ShapeDtypeStruct((3, 1, BLOCK, BLOCK), f32),
        ),
        in_specs=[pl.BlockSpec(memory_space=pl.ANY)] * 9,
        out_specs=[vmem] * 5,
        scratch_shapes=[
            pltpu.SMEM(structure.shape, jnp.int32),
            pltpu.SMEM(pick_second.shape, jnp.int32),
            pltpu.SMEM(pick_third.shape, jnp.int32),
            pltpu.VMEM((3, rows, BLOCK), f32),
            pltpu.VMEM(ancestor.shape, f32),
            pltpu.VMEM(diag_inverse.shape, f32),
            dma((9,)),
            pltpu.VMEM((SIDE, rows, rows), f32),
            pltpu.VMEM((SIDE, rows, wide), f32),
            pltpu.VMEM((SIDE, rows, wide), jnp.bfloat16),
            pltpu.VMEM((SIDE, rows, wide), jnp.bfloat16),
            pltpu.VMEM((rows, wide), f32),
            pltpu.VMEM((SIDE, rows, wide), f32),
            pltpu.VMEM((SIDE, rows, wide), f32),
            pltpu.VMEM((rows, wide), f32),
            pltpu.VMEM((2, 3, BLOCK, BLOCK), f32),
            pltpu.VMEM((3, BLOCK, BLOCK), f32),
            pltpu.VMEM((3, BLOCK, BLOCK), f32),
            pltpu.VMEM((3, BLOCK, BLOCK), f32),
            pltpu.VMEM((2, 3, BLOCK, BLOCK), f32),
            dma((most, CHUNKS)),
            dma((SIDE - 1, CHUNKS)),
            dma((SIDE,)),
            dma((SIDE,)),
            dma((SIDE,)),
            dma((SIDE,)),
            dma,
            dma((3,)),
            dma((3,)),
        ],
        compiler_params=pltpu.CompilerParams(
            collective_id=0, has_side_effects=True, vmem_limit_bytes=60 * 1024 * 1024
        ),
    )(
        structure, pick_second, pick_third, known_inverse, lower_first, lower_second, lower_third,
        ancestor, diag_inverse,
    )


def solution(mesh):
    fused = mesh.shape["row"] == SIDE and mesh.shape["col"] == SIDE
    placed = (
        P(("pole", "row"), "col"),
        P(("pole", "row"), "col"),
        P(("pole", "row"), "col"),
        P(("pole", "row"), "col"),
        P(("pole", "col"), None, None, None),
        P("pole", "col", None, None),
        P(),
        P(),
        P(),
    )
    return jax.shard_map(
        on_device_fused if fused else on_device,
        mesh=mesh,
        in_specs=placed,
        out_specs=(
            P(("pole", "row"), "col"),
            P(("pole", "row"), "col"),
            P(("pole", "row"), "col"),
            P(("pole", "col"), None, None, None),
            P("pole", "col", None, None),
        ),
        check_vma=False,
    )
```

```python
import jax
import jax.numpy as jnp
from jax import lax
from jax.experimental import pallas as pl
from jax.experimental.pallas import tpu as pltpu
from jax.sharding import PartitionSpec as P

HIGHEST = lax.Precision.HIGHEST


def broadcast(array, axis, root):
    mine = lax.axis_index(axis) == root
    return lax.psum(jnp.where(mine, array, jnp.zeros_like(array)), axis)


def block_mask(members, block_count):
    block_ids = jnp.arange(block_count, dtype=jnp.int32)
    return jnp.sum((members[:, :, None] == block_ids[None, None, :]).astype(jnp.float32), axis=1)


def structure_masks(structure, pick_second, pick_third, block_count):
    second_ids = jnp.take_along_axis(structure, pick_second, axis=1)
    third_ids = jnp.take_along_axis(second_ids, pick_third, axis=1)
    return (
        block_mask(structure, block_count),
        block_mask(second_ids, block_count),
        block_mask(third_ids, block_count),
    )


def expand_mask(mask_table, block_size):
    return jnp.repeat(jnp.repeat(mask_table.T, block_size, axis=0), block_size, axis=1)


def node_times(columns, blocks):
    height = columns.shape[0]
    node_count = blocks.shape[0]
    block_size = blocks.shape[1]
    reshaped = columns.reshape(height, node_count, block_size)
    return jnp.einsum("rkb,kbc->rkc", reshaped, blocks, precision=HIGHEST).reshape(
        height, node_count * block_size
    )


def node_inner(former, latter, block_size):
    height = former.shape[0]
    node_count = former.shape[1] // block_size
    return jnp.einsum(
        "rkb,rkc->kbc",
        former.reshape(height, node_count, block_size),
        latter.reshape(height, node_count, block_size),
        precision=HIGHEST,
    )


def block_product(former, latter):
    return jnp.einsum("kbc,kcd->kbd", former, latter, precision=HIGHEST)


def block_tproduct(former, latter):
    return jnp.einsum("kcb,kcd->kbd", former, latter, precision=HIGHEST)


def row_total(partial_sum):
    return lax.psum(partial_sum, "row")


def on_device(
    known_inverse,
    lower_first,
    lower_second,
    lower_third,
    ancestor,
    diag_inverse,
    structure,
    pick_second,
    pick_third,
):
    block_size = ancestor.shape[2]
    row_group = lax.axis_size("row") // lax.axis_size("col")
    local_blocks = known_inverse.shape[0] // block_size
    block_count = local_blocks * lax.axis_size("row")
    local_nodes = ancestor.shape[0]
    masks = structure_masks(structure, pick_second, pick_third, block_count)
    block_start = lax.axis_index("row") * local_blocks
    node_start = lax.axis_index("col") * local_nodes
    expanded = [
        expand_mask(
            lax.dynamic_slice(mask_table, (node_start, block_start), (local_nodes, local_blocks)),
            block_size,
        )
        for mask_table in masks
    ]
    lowers = [
        factor * kept_rows
        for factor, kept_rows in zip((lower_first, lower_second, lower_third), expanded)
    ]
    products = []
    for masked in lowers:
        gathered = lax.all_gather(masked, "col", axis=1, tiled=True)
        pieces = [
            broadcast(gathered, "row", lax.axis_index("col") * row_group + offset)
            for offset in range(row_group)
        ]
        partial_value = jnp.dot(known_inverse, jnp.concatenate(pieces, axis=0), precision=HIGHEST)
        products.append(lax.psum_scatter(partial_value, "col", scatter_dimension=1, tiled=True))
    link_two = ancestor[:, 0]
    link_near = ancestor[:, 1]
    link_far = ancestor[:, 2]
    first_cols = -expanded[0] * products[0]
    diag_first = diag_inverse[0] - row_total(node_inner(lowers[0], first_cols, block_size))
    second_cols = -expanded[1] * (products[1] + node_times(first_cols, link_two))
    parent_part = lax.psum(node_inner(first_cols, lowers[1], block_size), "row")
    cross_two = -(parent_part + block_product(diag_first, link_two))
    diag_second = (
        diag_inverse[1]
        - row_total(node_inner(lowers[1], second_cols, block_size))
        - block_tproduct(link_two, cross_two)
    )
    third_cols = -expanded[2] * (
        products[2] + node_times(second_cols, link_near) + node_times(first_cols, link_far)
    )
    near_part, far_part = lax.psum(
        (
            node_inner(second_cols, lowers[2], block_size),
            node_inner(first_cols, lowers[2], block_size),
        ),
        "row",
    )
    cross_near = -(
        near_part + block_product(diag_second, link_near) + block_tproduct(cross_two, link_far)
    )
    cross_far = -(
        far_part + block_product(cross_two, link_near) + block_product(diag_first, link_far)
    )
    diag_third = (
        diag_inverse[2]
        - row_total(node_inner(lowers[2], third_cols, block_size))
        - block_tproduct(link_near, cross_near)
        - block_tproduct(link_far, cross_far)
    )
    ancestral = jnp.stack([cross_two, cross_near, cross_far], axis=1)
    diagonal = jnp.stack([diag_first, diag_second, diag_third], axis=0)
    return (first_cols, second_cols, third_cols, ancestral, diagonal)


SIDE = 4
BLOCK = 128
CHUNKS = 8
MESH = pl.DeviceIdType.MESH


def landing_plan():
    half = {
        (0, 0): [],
        (1, 0): [(2, 2, 0), (3, 2, 0), (1, 1, 2)],
        (2, 0): [(2, 1, 0)],
        (3, 0): [(2, 1, 0), (3, 1, 0)],
        (0, 1): [(0, 0, 0)],
        (1, 1): [],
        (2, 1): [(0, 0, 0), (2, 2, 0)],
        (3, 1): [(0, 0, 1), (2, 2, 0), (3, 3, 0)],
    }
    plan = {}
    for (row, col), slots in half.items():
        plan[row, col] = [(col, None, 0)] + slots
        plan[3 - row, 3 - col] = [(3 - col, None, 0)] + [
            (3 - other, 3 - source, late) for other, source, late in slots
        ]
    return plan


def transfers():
    plan = landing_plan()
    sends = {place: [] for place in plan}
    for (row, col), slots in plan.items():
        for slot, (other, source, late) in enumerate(slots):
            if slot == 0:
                continue
            held = [have[0] for have in plan[row, source]]
            assert other in held
            sends[row, source].append((held.index(other), (row, col), slot, late))
    return plan, sends


FOLDS = {(3, 1): 2, (0, 2): 1}


def product_sends(plan):
    return {
        (place, slot): entry[0]
        for place, slots in plan.items()
        for slot, entry in enumerate(slots)
        if entry[0] != place[0] and not (place in FOLDS and slot == 1)
    }


def factor_sends(plan):
    direct = {place: [] for place in plan}
    passes = {}
    for owner, col in plan:
        takers = [
            row for row in range(SIDE)
            if row != owner and any(entry[0] == owner for entry in plan[row, col])
        ]
        near = (owner + 2) % SIDE
        far = near + 1 - 2 * (near % 2)
        if near in takers and far in takers:
            takers.remove(far)
            assert (near, col) not in passes
            passes[near, col] = (owner, far)
        direct[owner, col] = takers
    return direct, passes


def lookup(me, values):
    total = jnp.int32(0)
    for place, value in values.items():
        if value:
            total = total + jnp.where(me == place[0] * SIDE + place[1], jnp.int32(value), jnp.int32(0))
    return total


def split(value):
    high = value.astype(jnp.bfloat16)
    low = (value - high.astype(jnp.float32)).astype(jnp.bfloat16)
    return high, low


def mul(a, b):
    return jnp.dot(a, b, preferred_element_type=jnp.float32)


def dot3(left, right):
    return mul(left[0], right[0]) + (mul(left[0], right[1]) + mul(left[1], right[0]))


def fused_kernel(
    structure_in, second_in, third_in, k_ref, l1_in, l2_in, l3_in, anc_in, dinv_in,
    first_ref, second_out, third_out, ancestral_ref, diagonal_ref,
    structure_ref, second_ref, third_ref, lbuf, anc_ref, dinv_ref, copied,
    kbuf, mf, mhi, mlo, acc, outm, pin, fold, part, got_core, half_sum, got_row, total,
    ksend, krecv, msend, mrecv, psend, precv, fsem, rsend, rrecv,
):
    row = lax.axis_index("row")
    col = lax.axis_index("col")
    me = row * SIDE + col
    plan, sends = transfers()
    rows_of = SIDE * BLOCK
    step_rows = rows_of // CHUNKS

    def at(place):
        return pl.when(me == place[0] * SIDE + place[1])

    def piece(chunk, diagonal):
        half = rows_of // 2
        low = diagonal and chunk * step_rows >= half
        columns = pl.ds(half, half) if low else pl.ds(0, rows_of)
        return pl.ds(chunk * step_rows, step_rows), columns

    def block_copy(index, source_slot, target, slot, chunk):
        area = piece(chunk, plan[target][slot][0] == target[0])
        source = k_ref.at[area] if source_slot == 0 else kbuf.at[(source_slot, *area)]
        return pltpu.make_async_remote_copy(
            src_ref=source,
            dst_ref=kbuf.at[(slot, *area)],
            send_sem=ksend.at[index, chunk],
            recv_sem=krecv.at[slot - 1, chunk],
            device_id={"col": target[1]},
            device_id_type=MESH,
        )

    def wait_block(slot, chunk, diagonal):
        area = piece(chunk, diagonal)
        pltpu.make_async_copy(
            k_ref.at[area], kbuf.at[(slot, *area)], krecv.at[slot - 1, chunk]
        ).wait()

    def fold_copy(taker):
        return pltpu.make_async_remote_copy(
            src_ref=outm.at[1],
            dst_ref=fold,
            send_sem=psend.at[1],
            recv_sem=fsem,
            device_id={"row": taker},
            device_id_type=MESH,
        )

    def wait_factor(owner):
        pltpu.make_async_copy(mf.at[owner], mf.at[owner], mrecv.at[owner]).wait()

    def factor_copy(owner, taker):
        return pltpu.make_async_remote_copy(
            src_ref=mf.at[owner],
            dst_ref=mf.at[owner],
            send_sem=msend.at[taker],
            recv_sem=mrecv.at[owner],
            device_id={"row": taker},
            device_id_type=MESH,
        )

    def product_copy(sender, slot, taker):
        return pltpu.make_async_remote_copy(
            src_ref=outm.at[slot],
            dst_ref=pin.at[sender],
            send_sem=psend.at[slot],
            recv_sem=precv.at[sender],
            device_id={"row": taker},
            device_id_type=MESH,
        )

    local = [
        pltpu.make_async_copy(source, target, copied.at[index])
        for index, (source, target) in enumerate([
            (structure_in, structure_ref), (second_in, second_ref), (third_in, third_ref),
            (l1_in, lbuf.at[0]), (l2_in, lbuf.at[1]), (l3_in, lbuf.at[2]),
            (k_ref, kbuf.at[0]), (anc_in, anc_ref), (dinv_in, dinv_ref),
        ])
    ]
    for copy in local:
        copy.start()

    barrier = pltpu.get_barrier_semaphore()
    for step in range(1, SIDE):
        pl.semaphore_signal(barrier, inc=1, device_id={"col": lax.rem(col + step, SIDE)}, device_id_type=MESH)
        pl.semaphore_signal(barrier, inc=1, device_id={"row": lax.rem(row + step, SIDE)}, device_id_type=MESH)
    pl.semaphore_wait(barrier, 2 * (SIDE - 1))

    for place, listed in sends.items():
        early = [(i, s) for i, s in enumerate(listed) if s[0] == 0 and not s[3]]
        if early:
            @at(place)
            def _(early=early):
                for chunk in range(CHUNKS):
                    for index, (source_slot, target, slot, _) in early:
                        block_copy(index, source_slot, target, slot, chunk).start()

    for copy in local[:6]:
        copy.wait()

    def marks(ids, block):
        total_mark = jnp.float32(0)
        for one in ids:
            total_mark = total_mark + jnp.where(one == block, jnp.float32(1), jnp.float32(0))
        return total_mark

    ids_1 = [structure_ref[col, i] for i in range(structure_ref.shape[1])]
    ids_2 = [structure_ref[col, second_ref[col, i]] for i in range(second_ref.shape[1])]
    ids_3 = [
        structure_ref[col, second_ref[col, third_ref[col, i]]] for i in range(third_ref.shape[1])
    ]
    keep = [[marks(ids, row * SIDE + i) for i in range(SIDE)] for ids in (ids_1, ids_2, ids_3)]
    for level in range(3):
        for i in range(SIDE):
            rows = slice(i * BLOCK, (i + 1) * BLOCK)
            columns = slice(level * BLOCK, (level + 1) * BLOCK)
            mf[row, rows, columns] = lbuf[level, rows, :] * keep[level][i]

    direct, passes = factor_sends(plan)
    products = product_sends(plan)
    for place, takers in direct.items():
        if takers:
            @at(place)
            def _(place=place, takers=takers):
                for taker in takers:
                    factor_copy(place[0], taker).start()

    acc[...] = jnp.zeros_like(acc)

    def split_factor(index):
        def body(t, carry):
            rows = pl.ds(pl.multiple_of(t * BLOCK, BLOCK), BLOCK)
            high, low = split(mf[index, rows, :])
            mhi[index, rows, :] = high
            mlo[index, rows, :] = low
            return carry
        lax.fori_loop(0, SIDE, body, 0)

    split_factor(row)

    def relay(chunks, slots_passed):
        for place, listed in sends.items():
            passed = [(i, s) for i, s in enumerate(listed) if s[0] in slots_passed]
            if passed:
                @at(place)
                def _(passed=passed, place=place):
                    for chunk in chunks:
                        for index, (source_slot, target, slot, _) in passed:
                            wait_block(source_slot, chunk, plan[place][source_slot][0] == place[0])
                            block_copy(index, source_slot, target, slot, chunk).start()

    for copy in local[6:]:
        copy.wait()

    has_slot = [lookup(me, {p: int(len(s) > slot) for p, s in plan.items()}) for slot in range(SIDE)]
    other_of = [
        lookup(me, {p: s[slot][0] for p, s in plan.items() if len(s) > slot}) for slot in range(SIDE)
    ]

    def arrive(slot):
        relayed = {p: int(any(s[0] == slot for s in listed)) for p, listed in sends.items()}
        fresh = has_slot[slot] - lookup(me, relayed)

        @pl.when((fresh == 1) & (other_of[slot] != row))
        def _():
            for chunk in range(CHUNKS):
                wait_block(slot, chunk, False)

        @pl.when((fresh == 1) & (other_of[slot] == row))
        def _():
            for chunk in range(CHUNKS):
                wait_block(slot, chunk, True)

    def message(slot):
        @pl.when((has_slot[slot] == 1) & (other_of[slot] != row))
        def _():
            def body(t, carry):
                part_of = pl.ds(pl.multiple_of(t * BLOCK, BLOCK), BLOCK)
                turned = split(kbuf[slot, :, part_of].T)
                outm[slot, part_of, :] = dot3(turned, (mhi[row], mlo[row]))
                return carry
            lax.fori_loop(0, SIDE, body, 0)

        if slot == 1:
            for place, taker in FOLDS.items():
                @at(place)
                def _(taker=taker):
                    fold_copy(taker).start()

                @at((taker, place[1]))
                def _():
                    pltpu.make_async_copy(outm.at[1], fold, fsem).wait()
                    outm[1] += fold[...]

        for (place, at_slot), taker in products.items():
            if at_slot == slot:
                @at(place)
                def _(place=place, taker=taker):
                    product_copy(place[0], slot, taker).start()

    def collect(slot):
        other = other_of[slot]

        passed = lookup(me, {
            p: 1 for p, (owner, _) in passes.items()
            if len(plan[p]) > slot and plan[p][slot][0] == owner
        })

        @pl.when((has_slot[slot] == 1) & (other != row) & (passed == 0))
        def _():
            wait_factor(other)

        @pl.when((has_slot[slot] == 1) & (other != row))
        def _():
            split_factor(other)

        if slot > 0:
            @pl.when((has_slot[slot] == 1) & (other == row))
            def _():
                half = rows_of // 2
                kbuf[slot, half:, :half] = kbuf[slot, :half, half:].T

        @pl.when(has_slot[slot] == 1)
        def _():
            def body(t, carry):
                part_of = pl.ds(pl.multiple_of(t * BLOCK, BLOCK), BLOCK)
                straight = split(kbuf[slot, part_of, :])
                acc[part_of, :] += dot3(straight, (mhi[other], mlo[other]))
                return carry
            lax.fori_loop(0, SIDE, body, 0)

    def start_late(stage):
        for place, listed in sends.items():
            late = [(i, s) for i, s in enumerate(listed) if s[3] == stage]
            if late:
                @at(place)
                def _(late=late):
                    for chunk in range(CHUNKS):
                        for index, (source_slot, target, slot, _) in late:
                            block_copy(index, source_slot, target, slot, chunk).start()

    every = range(1, SIDE)
    message(0)
    relay(range(0, 3), every)
    for place, (owner, taker) in passes.items():
        @at(place)
        def _(owner=owner, taker=taker, place=place):
            wait_factor(owner)
            pltpu.make_async_remote_copy(
                src_ref=mf.at[owner],
                dst_ref=mf.at[owner],
                send_sem=msend.at[place[0]],
                recv_sem=mrecv.at[owner],
                device_id={"row": taker},
                device_id_type=MESH,
            ).start()
    relay(range(3, 4), every)
    collect(0)
    start_late(1)
    relay(range(4, 6), every)
    relay(range(6, CHUNKS), [1])
    arrive(1)
    message(1)
    relay(range(6, 7), [2, 3])
    collect(1)
    relay(range(7, CHUNKS), [2, 3])
    arrive(2)
    message(2)
    collect(2)
    arrive(3)
    message(3)
    collect(3)

    for sender in range(SIDE):
        gets = lookup(me, {
            p: 1 for p in plan
            if any(q == (sender, p[1]) and taker == p[0] for (q, _), taker in products.items())
        })

        @pl.when(gets == 1)
        def _(sender=sender):
            pltpu.make_async_copy(outm.at[0], pin.at[sender], precv.at[sender]).wait()
            acc[...] += pin[sender]

    start_late(2)

    def kept(value, level):
        return jnp.concatenate(
            [-(value[i * BLOCK:(i + 1) * BLOCK, :] * keep[level][i]) for i in range(SIDE)], axis=0
        )

    factors = (mhi[row], mlo[row])
    links = [split(anc_ref[0, i]) for i in range(3)]
    first = kept(acc[:, 0:BLOCK], 0)
    first_ref[...] = first
    first_split = split(first)
    inner_first = dot3(split(first.T), factors)
    part[0, 0] = inner_first[:, 0:BLOCK].T
    part[0, 1] = inner_first[:, BLOCK:2 * BLOCK]
    part[0, 2] = inner_first[:, 2 * BLOCK:]
    second = kept(acc[:, BLOCK:2 * BLOCK] + dot3(first_split, links[0]), 1)
    second_out[...] = second
    later = (factors[0][:, BLOCK:], factors[1][:, BLOCK:])
    inner_second = dot3(split(second.T), later)
    part[1, 0] = inner_second[:, 0:BLOCK].T
    part[1, 1] = inner_second[:, BLOCK:]
    third = kept(
        acc[:, 2 * BLOCK:] + dot3(split(second), links[1]) + dot3(first_split, links[2]), 2
    )
    third_out[...] = third
    last = (factors[0][:, 2 * BLOCK:], factors[1][:, 2 * BLOCK:])
    part[1, 2] = dot3(split(third.T), last).T

    mine = lax.rem(row, 2)
    sibling = row + 1 - 2 * mine
    across = lax.rem(row + 2, SIDE)

    def exchange(source, target, index, partner):
        copy = pltpu.make_async_remote_copy(
            src_ref=source,
            dst_ref=target,
            send_sem=rsend.at[index],
            recv_sem=rrecv.at[index],
            device_id={"row": partner},
            device_id_type=MESH,
        )
        copy.start()
        return copy

    copy = exchange(part.at[1 - mine], got_core, 0, sibling)
    copy.wait()
    half_sum[...] = part[mine] + got_core[...]
    copy = exchange(half_sum, got_row, 1, across)
    copy.wait()
    total[mine] = half_sum[...] + got_row[...]
    copy = exchange(total.at[mine], total.at[mine], 2, sibling)
    copy.wait()

    turned = [split(anc_ref[0, i].T) for i in range(3)]
    diag_1 = dinv_ref[0, 0] - total[0, 0]
    diag_1s = split(diag_1)
    cross = -(total[0, 1] + dot3(diag_1s, links[0]))
    cross_s = split(cross)
    diag_2 = dinv_ref[1, 0] - total[1, 0] - dot3(turned[0], cross_s)
    near = -(total[1, 1] + dot3(split(diag_2), links[1]) + dot3(split(cross.T), links[2]))
    far = -(total[0, 2] + dot3(cross_s, links[1]) + dot3(diag_1s, links[2]))
    diag_3 = dinv_ref[2, 0] - total[1, 2] - dot3(turned[1], split(near)) - dot3(turned[2], split(far))
    ancestral_ref[0, 0] = cross
    ancestral_ref[0, 1] = near
    ancestral_ref[0, 2] = far
    diagonal_ref[0, 0] = diag_1
    diagonal_ref[1, 0] = diag_2
    diagonal_ref[2, 0] = diag_3

    for place, listed in sends.items():
        @at(place)
        def _(place=place, listed=listed):
            for index, (source_slot, target, slot, _) in enumerate(listed):
                for chunk in range(CHUNKS):
                    block_copy(index, source_slot, target, slot, chunk).wait_send()
            for taker in direct[place]:
                factor_copy(place[0], taker).wait_send()
            if place in passes:
                pltpu.make_async_copy(mf.at[0], mf.at[0], msend.at[place[0]]).wait()
            if place in FOLDS:
                fold_copy(FOLDS[place]).wait_send()
            for (origin, slot), taker in products.items():
                if origin == place:
                    product_copy(place[0], slot, taker).wait_send()


def store_kernel(*refs):
    sems = refs[10]
    copies = [pltpu.make_async_copy(refs[i], refs[i + 5], sems.at[i]) for i in range(5)]
    for copy in copies:
        copy.start()
    for copy in copies:
        copy.wait()


def on_device_fused(
    known_inverse, lower_first, lower_second, lower_third, ancestor, diag_inverse,
    structure, pick_second, pick_third,
):
    rows = SIDE * BLOCK
    wide = 3 * BLOCK
    f32 = jnp.float32
    most = max(len(listed) for listed in transfers()[1].values())
    vmem = pl.BlockSpec(memory_space=pltpu.VMEM)
    dma = pltpu.SemaphoreType.DMA
    results = pl.pallas_call(
        fused_kernel,
        out_shape=(
            jax.ShapeDtypeStruct((rows, BLOCK), f32),
            jax.ShapeDtypeStruct((rows, BLOCK), f32),
            jax.ShapeDtypeStruct((rows, BLOCK), f32),
            jax.ShapeDtypeStruct((1, 3, BLOCK, BLOCK), f32),
            jax.ShapeDtypeStruct((3, 1, BLOCK, BLOCK), f32),
        ),
        in_specs=[pl.BlockSpec(memory_space=pl.ANY)] * 9,
        out_specs=[vmem] * 5,
        scratch_shapes=[
            pltpu.SMEM(structure.shape, jnp.int32),
            pltpu.SMEM(pick_second.shape, jnp.int32),
            pltpu.SMEM(pick_third.shape, jnp.int32),
            pltpu.VMEM((3, rows, BLOCK), f32),
            pltpu.VMEM(ancestor.shape, f32),
            pltpu.VMEM(diag_inverse.shape, f32),
            dma((9,)),
            pltpu.VMEM((SIDE, rows, rows), f32),
            pltpu.VMEM((SIDE, rows, wide), f32),
            pltpu.VMEM((SIDE, rows, wide), jnp.bfloat16),
            pltpu.VMEM((SIDE, rows, wide), jnp.bfloat16),
            pltpu.VMEM((rows, wide), f32),
            pltpu.VMEM((SIDE, rows, wide), f32),
            pltpu.VMEM((SIDE, rows, wide), f32),
            pltpu.VMEM((rows, wide), f32),
            pltpu.VMEM((2, 3, BLOCK, BLOCK), f32),
            pltpu.VMEM((3, BLOCK, BLOCK), f32),
            pltpu.VMEM((3, BLOCK, BLOCK), f32),
            pltpu.VMEM((3, BLOCK, BLOCK), f32),
            pltpu.VMEM((2, 3, BLOCK, BLOCK), f32),
            dma((most, CHUNKS)),
            dma((SIDE - 1, CHUNKS)),
            dma((SIDE,)),
            dma((SIDE,)),
            dma((SIDE,)),
            dma((SIDE,)),
            dma,
            dma((3,)),
            dma((3,)),
        ],
        compiler_params=pltpu.CompilerParams(
            collective_id=0, has_side_effects=True, vmem_limit_bytes=60 * 1024 * 1024
        ),
    )(
        structure, pick_second, pick_third, known_inverse, lower_first, lower_second, lower_third,
        ancestor, diag_inverse,
    )
    anywhere = pl.BlockSpec(memory_space=pl.ANY)
    return pl.pallas_call(
        store_kernel,
        out_shape=tuple(jax.ShapeDtypeStruct(one.shape, one.dtype) for one in results),
        in_specs=[anywhere] * 5,
        out_specs=[anywhere] * 5,
        scratch_shapes=[dma((5,))],
        compiler_params=pltpu.CompilerParams(vmem_limit_bytes=60 * 1024 * 1024),
    )(*results)


def solution(mesh):
    fused = mesh.shape["row"] == SIDE and mesh.shape["col"] == SIDE
    placed = (
        P(("pole", "row"), "col"),
        P(("pole", "row"), "col"),
        P(("pole", "row"), "col"),
        P(("pole", "row"), "col"),
        P(("pole", "col"), None, None, None),
        P("pole", "col", None, None),
        P(),
        P(),
        P(),
    )
    return jax.shard_map(
        on_device_fused if fused else on_device,
        mesh=mesh,
        in_specs=placed,
        out_specs=(
            P(("pole", "row"), "col"),
            P(("pole", "row"), "col"),
            P(("pole", "row"), "col"),
            P(("pole", "col"), None, None, None),
            P("pole", "col", None, None),
        ),
        check_vma=False,
    )
```

```python
import jax
import jax.numpy as jnp
from jax import lax
from jax.experimental import pallas as pl
from jax.experimental.pallas import tpu as pltpu
from jax.sharding import PartitionSpec as P

HIGHEST = lax.Precision.HIGHEST


def broadcast(array, axis, root):
    mine = lax.axis_index(axis) == root
    return lax.psum(jnp.where(mine, array, jnp.zeros_like(array)), axis)


def block_mask(members, block_count):
    block_ids = jnp.arange(block_count, dtype=jnp.int32)
    return jnp.sum((members[:, :, None] == block_ids[None, None, :]).astype(jnp.float32), axis=1)


def structure_masks(structure, pick_second, pick_third, block_count):
    second_ids = jnp.take_along_axis(structure, pick_second, axis=1)
    third_ids = jnp.take_along_axis(second_ids, pick_third, axis=1)
    return (
        block_mask(structure, block_count),
        block_mask(second_ids, block_count),
        block_mask(third_ids, block_count),
    )


def expand_mask(mask_table, block_size):
    return jnp.repeat(jnp.repeat(mask_table.T, block_size, axis=0), block_size, axis=1)


def node_times(columns, blocks):
    height = columns.shape[0]
    node_count = blocks.shape[0]
    block_size = blocks.shape[1]
    reshaped = columns.reshape(height, node_count, block_size)
    return jnp.einsum("rkb,kbc->rkc", reshaped, blocks, precision=HIGHEST).reshape(
        height, node_count * block_size
    )


def node_inner(former, latter, block_size):
    height = former.shape[0]
    node_count = former.shape[1] // block_size
    return jnp.einsum(
        "rkb,rkc->kbc",
        former.reshape(height, node_count, block_size),
        latter.reshape(height, node_count, block_size),
        precision=HIGHEST,
    )


def block_product(former, latter):
    return jnp.einsum("kbc,kcd->kbd", former, latter, precision=HIGHEST)


def block_tproduct(former, latter):
    return jnp.einsum("kcb,kcd->kbd", former, latter, precision=HIGHEST)


def row_total(partial_sum):
    return lax.psum(partial_sum, "row")


def on_device(
    known_inverse,
    lower_first,
    lower_second,
    lower_third,
    ancestor,
    diag_inverse,
    structure,
    pick_second,
    pick_third,
):
    block_size = ancestor.shape[2]
    row_group = lax.axis_size("row") // lax.axis_size("col")
    local_blocks = known_inverse.shape[0] // block_size
    block_count = local_blocks * lax.axis_size("row")
    local_nodes = ancestor.shape[0]
    masks = structure_masks(structure, pick_second, pick_third, block_count)
    block_start = lax.axis_index("row") * local_blocks
    node_start = lax.axis_index("col") * local_nodes
    expanded = [
        expand_mask(
            lax.dynamic_slice(mask_table, (node_start, block_start), (local_nodes, local_blocks)),
            block_size,
        )
        for mask_table in masks
    ]
    lowers = [
        factor * kept_rows
        for factor, kept_rows in zip((lower_first, lower_second, lower_third), expanded)
    ]
    products = []
    for masked in lowers:
        gathered = lax.all_gather(masked, "col", axis=1, tiled=True)
        pieces = [
            broadcast(gathered, "row", lax.axis_index("col") * row_group + offset)
            for offset in range(row_group)
        ]
        partial_value = jnp.dot(known_inverse, jnp.concatenate(pieces, axis=0), precision=HIGHEST)
        products.append(lax.psum_scatter(partial_value, "col", scatter_dimension=1, tiled=True))
    link_two = ancestor[:, 0]
    link_near = ancestor[:, 1]
    link_far = ancestor[:, 2]
    first_cols = -expanded[0] * products[0]
    diag_first = diag_inverse[0] - row_total(node_inner(lowers[0], first_cols, block_size))
    second_cols = -expanded[1] * (products[1] + node_times(first_cols, link_two))
    parent_part = lax.psum(node_inner(first_cols, lowers[1], block_size), "row")
    cross_two = -(parent_part + block_product(diag_first, link_two))
    diag_second = (
        diag_inverse[1]
        - row_total(node_inner(lowers[1], second_cols, block_size))
        - block_tproduct(link_two, cross_two)
    )
    third_cols = -expanded[2] * (
        products[2] + node_times(second_cols, link_near) + node_times(first_cols, link_far)
    )
    near_part, far_part = lax.psum(
        (
            node_inner(second_cols, lowers[2], block_size),
            node_inner(first_cols, lowers[2], block_size),
        ),
        "row",
    )
    cross_near = -(
        near_part + block_product(diag_second, link_near) + block_tproduct(cross_two, link_far)
    )
    cross_far = -(
        far_part + block_product(cross_two, link_near) + block_product(diag_first, link_far)
    )
    diag_third = (
        diag_inverse[2]
        - row_total(node_inner(lowers[2], third_cols, block_size))
        - block_tproduct(link_near, cross_near)
        - block_tproduct(link_far, cross_far)
    )
    ancestral = jnp.stack([cross_two, cross_near, cross_far], axis=1)
    diagonal = jnp.stack([diag_first, diag_second, diag_third], axis=0)
    return (first_cols, second_cols, third_cols, ancestral, diagonal)


SIDE = 4
BLOCK = 128
CHUNKS = 8
MESH = pl.DeviceIdType.MESH


def landing_plan():
    half = {
        (0, 0): [],
        (1, 0): [(2, 2, 0), (3, 2, 0), (1, 1, 2)],
        (2, 0): [(2, 1, 0)],
        (3, 0): [(2, 1, 0), (3, 1, 0)],
        (0, 1): [(0, 0, 0)],
        (1, 1): [],
        (2, 1): [(0, 0, 0), (2, 2, 0)],
        (3, 1): [(0, 0, 1), (2, 2, 0), (3, 3, 0)],
    }
    plan = {}
    for (row, col), slots in half.items():
        plan[row, col] = [(col, None, 0)] + slots
        plan[3 - row, 3 - col] = [(3 - col, None, 0)] + [
            (3 - other, 3 - source, late) for other, source, late in slots
        ]
    return plan


def transfers():
    plan = landing_plan()
    sends = {place: [] for place in plan}
    for (row, col), slots in plan.items():
        for slot, (other, source, late) in enumerate(slots):
            if slot == 0:
                continue
            held = [have[0] for have in plan[row, source]]
            assert other in held
            sends[row, source].append((held.index(other), (row, col), slot, late))
    return plan, sends


FOLDS = {(3, 1): 2, (0, 2): 1}


def product_sends(plan):
    return {
        (place, slot): entry[0]
        for place, slots in plan.items()
        for slot, entry in enumerate(slots)
        if entry[0] != place[0] and not (place in FOLDS and slot == 1)
    }


def factor_sends(plan):
    direct = {place: [] for place in plan}
    passes = {}
    for owner, col in plan:
        takers = [
            row for row in range(SIDE)
            if row != owner and any(entry[0] == owner for entry in plan[row, col])
        ]
        near = (owner + 2) % SIDE
        far = near + 1 - 2 * (near % 2)
        if near in takers and far in takers:
            takers.remove(far)
            assert (near, col) not in passes
            passes[near, col] = (owner, far)
        direct[owner, col] = takers
    return direct, passes


def lookup(me, values):
    total = jnp.int32(0)
    for place, value in values.items():
        if value:
            total = total + jnp.where(me == place[0] * SIDE + place[1], jnp.int32(value), jnp.int32(0))
    return total


def split(value):
    high = value.astype(jnp.bfloat16)
    low = (value - high.astype(jnp.float32)).astype(jnp.bfloat16)
    return high, low


def mul(a, b):
    return jnp.dot(a, b, preferred_element_type=jnp.float32)


def dot3(left, right):
    return mul(left[0], right[0]) + (mul(left[0], right[1]) + mul(left[1], right[0]))


def fused_kernel(
    structure_in, second_in, third_in, k_ref, l1_in, l2_in, l3_in, anc_in, dinv_in,
    first_ref, second_out, third_out, ancestral_ref, diagonal_ref,
    structure_ref, second_ref, third_ref, lbuf, anc_ref, dinv_ref, copied,
    kbuf, mf, mhi, mlo, acc, outm, pin, fold, part, got_core, half_sum, got_row, total,
    ksend, krecv, msend, mrecv, psend, precv, fsem, rsend, rrecv,
):
    row = lax.axis_index("row")
    col = lax.axis_index("col")
    me = row * SIDE + col
    plan, sends = transfers()
    rows_of = SIDE * BLOCK
    step_rows = rows_of // CHUNKS

    def at(place):
        return pl.when(me == place[0] * SIDE + place[1])

    def piece(chunk, diagonal):
        half = rows_of // 2
        low = diagonal and chunk * step_rows >= half
        columns = pl.ds(half, half) if low else pl.ds(0, rows_of)
        return pl.ds(chunk * step_rows, step_rows), columns

    def block_copy(index, source_slot, target, slot, chunk):
        area = piece(chunk, plan[target][slot][0] == target[0])
        source = k_ref.at[area] if source_slot == 0 else kbuf.at[(source_slot, *area)]
        return pltpu.make_async_remote_copy(
            src_ref=source,
            dst_ref=kbuf.at[(slot, *area)],
            send_sem=ksend.at[index, chunk],
            recv_sem=krecv.at[slot - 1, chunk],
            device_id={"col": target[1]},
            device_id_type=MESH,
        )

    def wait_block(slot, chunk, diagonal):
        area = piece(chunk, diagonal)
        pltpu.make_async_copy(
            k_ref.at[area], kbuf.at[(slot, *area)], krecv.at[slot - 1, chunk]
        ).wait()

    def fold_copy(taker):
        return pltpu.make_async_remote_copy(
            src_ref=outm.at[1],
            dst_ref=fold,
            send_sem=psend.at[1],
            recv_sem=fsem,
            device_id={"row": taker},
            device_id_type=MESH,
        )

    def wait_factor(owner):
        pltpu.make_async_copy(mf.at[owner], mf.at[owner], mrecv.at[owner]).wait()

    def factor_copy(owner, taker):
        return pltpu.make_async_remote_copy(
            src_ref=mf.at[owner],
            dst_ref=mf.at[owner],
            send_sem=msend.at[taker],
            recv_sem=mrecv.at[owner],
            device_id={"row": taker},
            device_id_type=MESH,
        )

    def product_copy(sender, slot, taker):
        return pltpu.make_async_remote_copy(
            src_ref=outm.at[slot],
            dst_ref=pin.at[sender],
            send_sem=psend.at[slot],
            recv_sem=precv.at[sender],
            device_id={"row": taker},
            device_id_type=MESH,
        )

    local = [
        pltpu.make_async_copy(source, target, copied.at[index])
        for index, (source, target) in enumerate([
            (structure_in, structure_ref), (second_in, second_ref), (third_in, third_ref),
            (l1_in, lbuf.at[0]), (l2_in, lbuf.at[1]), (l3_in, lbuf.at[2]),
            (k_ref, kbuf.at[0]), (anc_in, anc_ref), (dinv_in, dinv_ref),
        ])
    ]
    for copy in local:
        copy.start()

    barrier = pltpu.get_barrier_semaphore()
    for step in range(1, SIDE):
        pl.semaphore_signal(barrier, inc=1, device_id={"col": lax.rem(col + step, SIDE)}, device_id_type=MESH)
        pl.semaphore_signal(barrier, inc=1, device_id={"row": lax.rem(row + step, SIDE)}, device_id_type=MESH)
    pl.semaphore_wait(barrier, 2 * (SIDE - 1))

    for place, listed in sends.items():
        early = [(i, s) for i, s in enumerate(listed) if s[0] == 0 and not s[3]]
        if early:
            @at(place)
            def _(early=early):
                for chunk in range(CHUNKS):
                    for index, (source_slot, target, slot, _) in early:
                        block_copy(index, source_slot, target, slot, chunk).start()

    for copy in local[:6]:
        copy.wait()

    def marks(ids, block):
        total_mark = jnp.float32(0)
        for one in ids:
            total_mark = total_mark + jnp.where(one == block, jnp.float32(1), jnp.float32(0))
        return total_mark

    ids_1 = [structure_ref[col, i] for i in range(structure_ref.shape[1])]
    ids_2 = [structure_ref[col, second_ref[col, i]] for i in range(second_ref.shape[1])]
    ids_3 = [
        structure_ref[col, second_ref[col, third_ref[col, i]]] for i in range(third_ref.shape[1])
    ]
    keep = [[marks(ids, row * SIDE + i) for i in range(SIDE)] for ids in (ids_1, ids_2, ids_3)]
    for level in range(3):
        for i in range(SIDE):
            rows = slice(i * BLOCK, (i + 1) * BLOCK)
            columns = slice(level * BLOCK, (level + 1) * BLOCK)
            mf[row, rows, columns] = lbuf[level, rows, :] * keep[level][i]

    direct, passes = factor_sends(plan)
    products = product_sends(plan)
    for place, takers in direct.items():
        if takers:
            @at(place)
            def _(place=place, takers=takers):
                for taker in takers:
                    factor_copy(place[0], taker).start()

    acc[...] = jnp.zeros_like(acc)

    def split_factor(index):
        def body(t, carry):
            rows = pl.ds(pl.multiple_of(t * BLOCK, BLOCK), BLOCK)
            high, low = split(mf[index, rows, :])
            mhi[index, rows, :] = high
            mlo[index, rows, :] = low
            return carry
        lax.fori_loop(0, SIDE, body, 0)

    split_factor(row)

    def relay(chunks, slots_passed):
        for place, listed in sends.items():
            passed = [(i, s) for i, s in enumerate(listed) if s[0] in slots_passed]
            if passed:
                @at(place)
                def _(passed=passed, place=place):
                    for chunk in chunks:
                        for index, (source_slot, target, slot, _) in passed:
                            wait_block(source_slot, chunk, plan[place][source_slot][0] == place[0])
                            block_copy(index, source_slot, target, slot, chunk).start()

    for copy in local[6:]:
        copy.wait()

    has_slot = [lookup(me, {p: int(len(s) > slot) for p, s in plan.items()}) for slot in range(SIDE)]
    other_of = [
        lookup(me, {p: s[slot][0] for p, s in plan.items() if len(s) > slot}) for slot in range(SIDE)
    ]

    def arrive(slot):
        relayed = {p: int(any(s[0] == slot for s in listed)) for p, listed in sends.items()}
        fresh = has_slot[slot] - lookup(me, relayed)

        @pl.when((fresh == 1) & (other_of[slot] != row))
        def _():
            for chunk in range(CHUNKS):
                wait_block(slot, chunk, False)

        @pl.when((fresh == 1) & (other_of[slot] == row))
        def _():
            for chunk in range(CHUNKS):
                wait_block(slot, chunk, True)

    def message(slot):
        @pl.when((has_slot[slot] == 1) & (other_of[slot] != row))
        def _():
            def body(t, carry):
                part_of = pl.ds(pl.multiple_of(t * BLOCK, BLOCK), BLOCK)
                turned = split(kbuf[slot, :, part_of].T)
                outm[slot, part_of, :] = dot3(turned, (mhi[row], mlo[row]))
                return carry
            lax.fori_loop(0, SIDE, body, 0)

        if slot == 1:
            for place, taker in FOLDS.items():
                @at(place)
                def _(taker=taker):
                    fold_copy(taker).start()

                @at((taker, place[1]))
                def _():
                    pltpu.make_async_copy(outm.at[1], fold, fsem).wait()
                    outm[1] += fold[...]

        for (place, at_slot), taker in products.items():
            if at_slot == slot:
                @at(place)
                def _(place=place, taker=taker):
                    product_copy(place[0], slot, taker).start()

    def collect(slot):
        other = other_of[slot]

        passed = lookup(me, {
            p: 1 for p, (owner, _) in passes.items()
            if len(plan[p]) > slot and plan[p][slot][0] == owner
        })

        @pl.when((has_slot[slot] == 1) & (other != row) & (passed == 0))
        def _():
            wait_factor(other)

        @pl.when((has_slot[slot] == 1) & (other != row))
        def _():
            split_factor(other)

        if slot > 0:
            @pl.when((has_slot[slot] == 1) & (other == row))
            def _():
                half = rows_of // 2
                kbuf[slot, half:, :half] = kbuf[slot, :half, half:].T

        @pl.when(has_slot[slot] == 1)
        def _():
            def body(t, carry):
                part_of = pl.ds(pl.multiple_of(t * BLOCK, BLOCK), BLOCK)
                straight = split(kbuf[slot, part_of, :])
                acc[part_of, :] += dot3(straight, (mhi[other], mlo[other]))
                return carry
            lax.fori_loop(0, SIDE, body, 0)

    def start_late(stage):
        for place, listed in sends.items():
            late = [(i, s) for i, s in enumerate(listed) if s[3] == stage]
            if late:
                @at(place)
                def _(late=late):
                    for chunk in range(CHUNKS):
                        for index, (source_slot, target, slot, _) in late:
                            block_copy(index, source_slot, target, slot, chunk).start()

    every = range(1, SIDE)
    message(0)
    relay(range(0, 3), every)
    for place, (owner, taker) in passes.items():
        @at(place)
        def _(owner=owner, taker=taker, place=place):
            wait_factor(owner)
            pltpu.make_async_remote_copy(
                src_ref=mf.at[owner],
                dst_ref=mf.at[owner],
                send_sem=msend.at[place[0]],
                recv_sem=mrecv.at[owner],
                device_id={"row": taker},
                device_id_type=MESH,
            ).start()
    relay(range(3, 4), every)
    collect(0)
    start_late(1)
    relay(range(4, 6), every)
    relay(range(6, CHUNKS), [1])
    arrive(1)
    message(1)
    relay(range(6, 7), [2, 3])
    collect(1)
    relay(range(7, CHUNKS), [2, 3])
    arrive(2)
    message(2)
    collect(2)
    arrive(3)
    message(3)
    collect(3)

    for sender in range(SIDE):
        gets = lookup(me, {
            p: 1 for p in plan
            if any(q == (sender, p[1]) and taker == p[0] for (q, _), taker in products.items())
        })

        @pl.when(gets == 1)
        def _(sender=sender):
            pltpu.make_async_copy(outm.at[0], pin.at[sender], precv.at[sender]).wait()
            acc[...] += pin[sender]

    start_late(2)

    def kept(value, level):
        return jnp.concatenate(
            [-(value[i * BLOCK:(i + 1) * BLOCK, :] * keep[level][i]) for i in range(SIDE)], axis=0
        )

    factors = (mhi[row], mlo[row])
    links = [split(anc_ref[0, i]) for i in range(3)]
    first = kept(acc[:, 0:BLOCK], 0)
    first_ref[...] = first
    first_split = split(first)
    inner_first = dot3(split(first.T), factors)
    part[0, 0] = inner_first[:, 0:BLOCK].T
    part[0, 1] = inner_first[:, BLOCK:2 * BLOCK]
    part[0, 2] = inner_first[:, 2 * BLOCK:]
    second = kept(acc[:, BLOCK:2 * BLOCK] + dot3(first_split, links[0]), 1)
    second_out[...] = second
    later = (factors[0][:, BLOCK:], factors[1][:, BLOCK:])
    inner_second = dot3(split(second.T), later)
    part[1, 0] = inner_second[:, 0:BLOCK].T
    part[1, 1] = inner_second[:, BLOCK:]
    third = kept(
        acc[:, 2 * BLOCK:] + dot3(split(second), links[1]) + dot3(first_split, links[2]), 2
    )
    third_out[...] = third
    last = (factors[0][:, 2 * BLOCK:], factors[1][:, 2 * BLOCK:])
    part[1, 2] = dot3(split(third.T), last).T

    mine = lax.rem(row, 2)
    sibling = row + 1 - 2 * mine
    across = lax.rem(row + 2, SIDE)

    def exchange(source, target, index, partner):
        copy = pltpu.make_async_remote_copy(
            src_ref=source,
            dst_ref=target,
            send_sem=rsend.at[index],
            recv_sem=rrecv.at[index],
            device_id={"row": partner},
            device_id_type=MESH,
        )
        copy.start()
        return copy

    copy = exchange(part.at[1 - mine], got_core, 0, sibling)
    copy.wait()
    half_sum[...] = part[mine] + got_core[...]
    copy = exchange(half_sum, got_row, 1, across)
    copy.wait()
    total[mine] = half_sum[...] + got_row[...]
    copy = exchange(total.at[mine], total.at[mine], 2, sibling)
    copy.wait()

    turned = [split(anc_ref[0, i].T) for i in range(3)]
    diag_1 = dinv_ref[0, 0] - total[0, 0]
    diag_1s = split(diag_1)
    cross = -(total[0, 1] + dot3(diag_1s, links[0]))
    cross_s = split(cross)
    diag_2 = dinv_ref[1, 0] - total[1, 0] - dot3(turned[0], cross_s)
    near = -(total[1, 1] + dot3(split(diag_2), links[1]) + dot3(split(cross.T), links[2]))
    far = -(total[0, 2] + dot3(cross_s, links[1]) + dot3(diag_1s, links[2]))
    diag_3 = dinv_ref[2, 0] - total[1, 2] - dot3(turned[1], split(near)) - dot3(turned[2], split(far))
    ancestral_ref[0, 0] = cross
    ancestral_ref[0, 1] = near
    ancestral_ref[0, 2] = far
    diagonal_ref[0, 0] = diag_1
    diagonal_ref[1, 0] = diag_2
    diagonal_ref[2, 0] = diag_3

    for place, listed in sends.items():
        @at(place)
        def _(place=place, listed=listed):
            for index, (source_slot, target, slot, _) in enumerate(listed):
                for chunk in range(CHUNKS):
                    block_copy(index, source_slot, target, slot, chunk).wait_send()
            for taker in direct[place]:
                factor_copy(place[0], taker).wait_send()
            if place in passes:
                pltpu.make_async_copy(mf.at[0], mf.at[0], msend.at[place[0]]).wait()
            if place in FOLDS:
                fold_copy(FOLDS[place]).wait_send()
            for (origin, slot), taker in products.items():
                if origin == place:
                    product_copy(place[0], slot, taker).wait_send()


def store_kernel(*refs):
    held, sems = refs[10:15], refs[15]
    loads = [pltpu.make_async_copy(refs[i], held[i], sems.at[i]) for i in range(5)]
    stores = [pltpu.make_async_copy(held[i], refs[i + 5], sems.at[i + 5]) for i in range(5)]
    for copy in loads:
        copy.start()
    for load, store in zip(loads, stores):
        load.wait()
        store.start()
    for copy in stores:
        copy.wait()


def on_device_fused(
    known_inverse, lower_first, lower_second, lower_third, ancestor, diag_inverse,
    structure, pick_second, pick_third,
):
    rows = SIDE * BLOCK
    wide = 3 * BLOCK
    f32 = jnp.float32
    most = max(len(listed) for listed in transfers()[1].values())
    vmem = pl.BlockSpec(memory_space=pltpu.VMEM)
    dma = pltpu.SemaphoreType.DMA
    results = pl.pallas_call(
        fused_kernel,
        out_shape=(
            jax.ShapeDtypeStruct((rows, BLOCK), f32),
            jax.ShapeDtypeStruct((rows, BLOCK), f32),
            jax.ShapeDtypeStruct((rows, BLOCK), f32),
            jax.ShapeDtypeStruct((1, 3, BLOCK, BLOCK), f32),
            jax.ShapeDtypeStruct((3, 1, BLOCK, BLOCK), f32),
        ),
        in_specs=[pl.BlockSpec(memory_space=pl.ANY)] * 9,
        out_specs=[vmem] * 5,
        scratch_shapes=[
            pltpu.SMEM(structure.shape, jnp.int32),
            pltpu.SMEM(pick_second.shape, jnp.int32),
            pltpu.SMEM(pick_third.shape, jnp.int32),
            pltpu.VMEM((3, rows, BLOCK), f32),
            pltpu.VMEM(ancestor.shape, f32),
            pltpu.VMEM(diag_inverse.shape, f32),
            dma((9,)),
            pltpu.VMEM((SIDE, rows, rows), f32),
            pltpu.VMEM((SIDE, rows, wide), f32),
            pltpu.VMEM((SIDE, rows, wide), jnp.bfloat16),
            pltpu.VMEM((SIDE, rows, wide), jnp.bfloat16),
            pltpu.VMEM((rows, wide), f32),
            pltpu.VMEM((SIDE, rows, wide), f32),
            pltpu.VMEM((SIDE, rows, wide), f32),
            pltpu.VMEM((rows, wide), f32),
            pltpu.VMEM((2, 3, BLOCK, BLOCK), f32),
            pltpu.VMEM((3, BLOCK, BLOCK), f32),
            pltpu.VMEM((3, BLOCK, BLOCK), f32),
            pltpu.VMEM((3, BLOCK, BLOCK), f32),
            pltpu.VMEM((2, 3, BLOCK, BLOCK), f32),
            dma((most, CHUNKS)),
            dma((SIDE - 1, CHUNKS)),
            dma((SIDE,)),
            dma((SIDE,)),
            dma((SIDE,)),
            dma((SIDE,)),
            dma,
            dma((3,)),
            dma((3,)),
        ],
        compiler_params=pltpu.CompilerParams(
            collective_id=0, has_side_effects=True, vmem_limit_bytes=60 * 1024 * 1024
        ),
    )(
        structure, pick_second, pick_third, known_inverse, lower_first, lower_second, lower_third,
        ancestor, diag_inverse,
    )
    anywhere = pl.BlockSpec(memory_space=pl.ANY)
    return pl.pallas_call(
        store_kernel,
        out_shape=tuple(jax.ShapeDtypeStruct(one.shape, one.dtype) for one in results),
        in_specs=[anywhere] * 5,
        out_specs=[anywhere] * 5,
        scratch_shapes=[pltpu.VMEM(one.shape, f32) for one in results] + [dma((10,))],
        compiler_params=pltpu.CompilerParams(vmem_limit_bytes=60 * 1024 * 1024),
    )(*results)


def solution(mesh):
    fused = mesh.shape["row"] == SIDE and mesh.shape["col"] == SIDE
    placed = (
        P(("pole", "row"), "col"),
        P(("pole", "row"), "col"),
        P(("pole", "row"), "col"),
        P(("pole", "row"), "col"),
        P(("pole", "col"), None, None, None),
        P("pole", "col", None, None),
        P(),
        P(),
        P(),
    )
    return jax.shard_map(
        on_device_fused if fused else on_device,
        mesh=mesh,
        in_specs=placed,
        out_specs=(
            P(("pole", "row"), "col"),
            P(("pole", "row"), "col"),
            P(("pole", "row"), "col"),
            P(("pole", "col"), None, None, None),
            P("pole", "col", None, None),
        ),
        check_vma=False,
    )
```
